32 devices in a mesh: section: 4 (over z), dp: 8 (over y, x, core).
Axes of the slice: x: 2, y: 2, z: 4, core: 2. Of those that a mesh axis runs over, the one named last changes fastest.
Arguments:
- out_grad: bfloat16 [2, 512, 6144], P(None, 'dp'), may hold values from -6 to 6
- x_rows: bfloat16 [4, 2, 16, 6144], P('section'), may hold values from -6 to 6
- saved_u: bfloat16 [4, 2, 16, 5376], P('section', None, None, 'dp'), may hold values from -6 to 6
- w_up_t: bfloat16 [4, 5376, 6144], P('section', 'dp'), may hold values from -0.078125 to 0.078125
- w_down: bfloat16 [4, 5376, 6144], P('section', 'dp'), may hold values from -0.078125 to 0.078125
- gate: float32 [4, 2, 16], P('section', None, 'dp'), may hold values from 0.2 to 1
- route_tokens: int32 [4, 2, 16], P('section', None, 'dp'), may hold values from 0 to 63
- route_count: int32 [4, 2, 8], P('section', None, 'dp'), may hold values from 1 to 2, as said below
Outputs:
- in_grad: bfloat16 [4, 2, 512, 6144], P('section', None, 'dp')
- grad_up_t: bfloat16 [4, 5376, 6144], P('section', 'dp')
- grad_down: bfloat16 [4, 5376, 6144], P('section', 'dp')
The draws below stay inside these ranges and needn't reach their ends.
Inputs may be any that keep to these rules, and one draw needn't show every extreme that they name: `route_tokens`: a token index within the micro-batch rows of the slot's dp index. `route_count`: in every layer and micro-batch some dp index has all 2 slots live.
All inputs are finite; a program needn't handle non-finite values.
Results may differ from the reference program's by a relative error of at most 0.0059.
Values may be sent and summed in bfloat16 or wider, within the bound.
A program may use at most 128 MiB of HBM per device.

```python
import math
import jax
import jax.numpy as jnp

D = 6144
HID = 5376
TOK_MB = 64
MICRO = 2
CAP = 2
LAYERS = 4
TOKENS = 512
ROWS = 16
N_SECTION = 4
N_DP = 8


def draw_route_count(key, part):
    key = jax.random.fold_in(key, 5)
    first_key, second_key = jax.random.split(key)
    counts = jax.random.randint(first_key, (N_SECTION, MICRO, N_DP), 1, CAP + 1)
    filled = jax.random.randint(second_key, (N_SECTION, MICRO, 1), 0, N_DP)
    positions = jnp.arange(N_DP)[None, None, :]
    return jnp.where(positions == filled, CAP, counts).astype(jnp.int32)


def place_ends(drawn, own_key, low, largest):
    place = [jax.random.randint(jax.random.fold_in(own_key, axis), (), 0, length) for axis, length in enumerate(drawn.shape)]
    main_axis = drawn.shape.index(max(drawn.shape))
    neighbour = place[:main_axis] + [(place[main_axis] + 1) % drawn.shape[main_axis]] + place[main_axis + 1:]
    return drawn.at[tuple(place)].set(low).at[tuple(neighbour)].set(largest)


def steps_of(own_key, shape, pieces, least, largest):
    gain = 1.0
    for position, blocks in pieces:
        heights = jax.random.uniform(jax.random.fold_in(jax.random.fold_in(own_key, 6), position), (blocks,), jnp.float32, least / len(pieces), largest / len(pieces))
        gain = gain * jnp.repeat(jnp.exp(heights), shape[position] // blocks).reshape((-1,) + (1,) * (len(shape) - 1 - position))
    return gain


def scatter_about(stream_key, shape, deviation, most, shards=(), held_as=jnp.bfloat16):
    values = jax.random.normal(stream_key, shape, jnp.float32) * deviation
    if len(shards) > 0:
        values = steps_of(stream_key, shape, shards, -0.22, 0.18) * values
    return jnp.clip(values, min=-most, max=most).astype(held_as)


def setup_inputs(seed: int = 0) -> dict:
    keys = jax.random.split(jax.random.key(seed), 9)
    return {
        "out_grad": scatter_about(keys[0], (MICRO, TOKENS, D), 1.0, 6.0, ((1, 8),)),
        "x_rows": scatter_about(keys[1], (LAYERS, MICRO, ROWS, D), 1.0, 6.0, ((0, 4),)),
        "saved_u": scatter_about(keys[2], (LAYERS, MICRO, ROWS, HID), 1.5, 6.0, ((0, 4), (3, 8))),
        "w_up_t": scatter_about(keys[3], (LAYERS, HID, D), D ** -0.5, 0.078125, ((0, 4), (1, 8))),
        "w_down": scatter_about(keys[4], (LAYERS, HID, D), HID ** -0.5, 0.078125, ((0, 4), (1, 8))),
        "gate": jnp.clip(jnp.exp(math.log(1.0) - 1.609438 * jax.random.uniform(keys[5], (LAYERS, MICRO, ROWS), jnp.float32) ** steps_of(keys[5], (LAYERS, MICRO, ROWS), ((0, 4), (2, 8)), -0.2, 0.2)), 0.2, 1.0),
        "route_tokens": place_ends(jax.random.randint(keys[6], (LAYERS, MICRO, ROWS), 0, TOK_MB), jax.random.fold_in(keys[6], 1), 0, TOK_MB - 1).astype(jnp.int32),
        "route_count": draw_route_count(jax.random.fold_in(keys[8], 71), 0),
    }


def silu_pair(pre_activation):
    sigmoid_v = jax.nn.sigmoid(pre_activation)
    return pre_activation * sigmoid_v, sigmoid_v * (1.0 + pre_activation * (1.0 - sigmoid_v))


def reference(out_grad, x_rows, saved_u, w_up_t, w_down, gate, route_tokens, route_count):
    slot_index = jnp.arange(ROWS, dtype=jnp.int32)
    owner_index = slot_index // CAP
    slabs = [out_grad[micro_index] for micro_index in range(MICRO)]
    in_grads = []
    ups = []
    downs = []
    for layer_index in range(LAYERS - 1, -1, -1):
        grad_down = jnp.zeros((HID, D), jnp.float32)
        grad_up = jnp.zeros((HID, D), jnp.float32)
        layer_grads = []
        for micro_index in range(MICRO):
            grad_slab = slabs[micro_index]
            token_ids = (owner_index * TOK_MB + route_tokens[layer_index, micro_index]).astype(jnp.int32)
            live_slots = (slot_index % CAP) < route_count[layer_index, micro_index][owner_index]
            weights = jnp.where(live_slots, gate[layer_index, micro_index], jnp.float32(0.0))
            scaled = (weights[:, None] * grad_slab[token_ids].astype(jnp.float32)).astype(jnp.bfloat16)
            activation_f, slope_factor = silu_pair(saved_u[layer_index, micro_index].astype(jnp.float32))
            activation = activation_f.astype(jnp.bfloat16)
            hidden_back = jnp.dot(scaled, w_down[layer_index].T, preferred_element_type=jnp.float32)
            hidden_grad = (hidden_back * slope_factor).astype(jnp.bfloat16)
            grad_down = grad_down + jnp.dot(activation.T, scaled, preferred_element_type=jnp.float32)
            grad_up = grad_up + jnp.dot(hidden_grad.T, x_rows[layer_index, micro_index], preferred_element_type=jnp.float32)
            row_grad = jnp.dot(hidden_grad, w_up_t[layer_index], preferred_element_type=jnp.float32)
            updated = grad_slab.astype(jnp.float32).at[token_ids].add(row_grad)
            slabs[micro_index] = updated.astype(jnp.bfloat16)
            layer_grads.append(slabs[micro_index])
        in_grads.append(jnp.stack(layer_grads))
        ups.append(grad_up.astype(jnp.bfloat16))
        downs.append(grad_down.astype(jnp.bfloat16))
    in_grads = in_grads[::-1]
    ups = ups[::-1]
    downs = downs[::-1]
    return jnp.stack(in_grads), jnp.stack(ups), jnp.stack(downs)
```

```python
import functools

import jax
import jax.numpy as jnp
from jax import lax
from jax.experimental import pallas as pl
from jax.experimental.pallas import tpu as pltpu
from jax.sharding import PartitionSpec as P

MESH = pl.DeviceIdType.MESH
TILE_ROWS = 16
GATHER_CHUNKS = 2
REDUCE_CHUNKS = 3


def chain_kernel(
    sizes,
    base_ref, weight_ref, id_col_ref, id_row_ref, id_send_ref, slope_ref, w_up_hbm, w_down_hbm,
    all_new_ref, all_ids_ref, gathered_ref, hidden_ref,
    w_up, w_down, gbuf, send_buf, recv_buf, new_buf, id_buf, cur_buf,
    weight_sem, gather_send, gather_recv, reduce_send, reduce_recv, id_send, id_recv, new_send, new_recv,
):
    sections, peers, fold, slots = sizes
    section = lax.axis_index("section")
    me = lax.axis_index("dp")
    width = gbuf.shape[1]
    hid = w_down.shape[0]
    rows = peers * TILE_ROWS

    down_copy = pltpu.make_async_copy(w_down_hbm, w_down, weight_sem.at[0])
    up_copy = pltpu.make_async_copy(w_up_hbm, w_up, weight_sem.at[1])
    down_copy.start()
    up_copy.start()

    def peer_at(k):
        return lax.rem(me + k, peers)

    barrier = pltpu.get_barrier_semaphore()

    def greet(k, carry):
        pl.semaphore_signal(barrier, inc=1, device_id=(section, peer_at(k)), device_id_type=MESH)
        return carry

    lax.fori_loop(1, peers, greet, 0)
    for k in range(1, sections):
        other = lax.rem(section + k, sections)
        pl.semaphore_signal(barrier, inc=1, device_id=(other, me), device_id_type=MESH)
    pl.semaphore_wait(barrier, peers - 1 + sections - 1)

    def id_copy(source, target):
        return pltpu.make_async_remote_copy(
            src_ref=id_send_ref, dst_ref=id_buf.at[source],
            send_sem=id_send.at[target], recv_sem=id_recv.at[source],
            device_id=(target, me), device_id_type=MESH)

    def new_copy(source, target):
        return pltpu.make_async_remote_copy(
            src_ref=new_buf.at[source], dst_ref=new_buf.at[source],
            send_sem=new_send.at[target], recv_sem=new_recv.at[source],
            device_id=(target, me), device_id_type=MESH)

    for target in range(sections - 1):
        @pl.when(target < section)
        def _():
            id_copy(section, target).start()

    cur_buf[...] = base_ref[...]
    id_col = id_col_ref[...]
    for upper in range(sections - 1, 0, -1):
        @pl.when(upper > section)
        def _():
            id_copy(upper, upper).wait_recv()
            new_copy(upper, upper).wait_recv()
            same = id_col[:, :TILE_ROWS] == id_buf[upper][:1, :TILE_ROWS]
            picks = jnp.where(same, 1.0, 0.0)
            hit = jnp.max(picks, axis=1, keepdims=True) > 0.5
            taken = jnp.dot(picks.astype(jnp.bfloat16), new_buf[upper], preferred_element_type=jnp.float32)
            cur_buf[...] = jnp.where(hit, taken, cur_buf[...].astype(jnp.float32)).astype(jnp.bfloat16)

    current = cur_buf[...].astype(jnp.float32)
    scaled = (weight_ref[...][:, :1] * current).astype(jnp.bfloat16)
    my_rows = pl.ds(pl.multiple_of(me * TILE_ROWS, TILE_ROWS), TILE_ROWS)
    gbuf[my_rows, :] = scaled

    g_width = width // GATHER_CHUNKS

    def gather_copy(chunk, source, target):
        place = (pl.ds(pl.multiple_of(source * TILE_ROWS, TILE_ROWS), TILE_ROWS), pl.ds(chunk * g_width, g_width))
        return pltpu.make_async_remote_copy(
            src_ref=gbuf.at[place], dst_ref=gbuf.at[place],
            send_sem=gather_send.at[chunk, target], recv_sem=gather_recv.at[chunk, source],
            device_id=(section, target), device_id_type=MESH)

    for chunk in range(GATHER_CHUNKS):
        def send(k, carry):
            gather_copy(chunk, me, peer_at(k)).start()
            return carry
        lax.fori_loop(1, peers, send, 0)

    down_copy.wait()
    lane_piece = lax.broadcasted_iota(jnp.int32, (hid, rows), 1) % TILE_ROWS // slots
    total = jnp.zeros((hid, rows), jnp.float32)
    for chunk in range(GATHER_CHUNKS):
        def arrive(k, carry):
            peer = peer_at(k)
            gather_copy(chunk, peer, peer).wait_recv()
            return carry
        lax.fori_loop(1, peers, arrive, 0)
        block = gbuf[:, chunk * g_width:(chunk + 1) * g_width]
        for piece in range(fold):
            start = piece * width + chunk * g_width
            product = lax.dot_general(
                w_down[:, start:start + g_width], block, (((1,), (1,)), ((), ())),
                preferred_element_type=jnp.float32)
            total = total + jnp.where(lane_piece == piece, product, 0.0)

    back = total.T.reshape(peers, TILE_ROWS, hid)
    summed = back
    for k in range(1, fold):
        cut = k * slots
        summed = summed + jnp.concatenate([back[:, cut:], back[:, :cut]], axis=1)
    hidden = (summed.reshape(rows, hid) * slope_ref[...]).astype(jnp.bfloat16)
    hidden_ref[...] = hidden

    r_width = width // REDUCE_CHUNKS

    def reduce_copy(chunk, source, target):
        columns = pl.ds(chunk * r_width, r_width)
        return pltpu.make_async_remote_copy(
            src_ref=send_buf.at[pl.ds(pl.multiple_of(target * TILE_ROWS, TILE_ROWS), TILE_ROWS), columns],
            dst_ref=recv_buf.at[pl.ds(pl.multiple_of(source * TILE_ROWS, TILE_ROWS), TILE_ROWS), columns],
            send_sem=reduce_send.at[chunk, target], recv_sem=reduce_recv.at[chunk, source],
            device_id=(section, target), device_id_type=MESH)

    up_copy.wait()
    row_piece = lax.broadcasted_iota(jnp.int32, (rows, r_width), 0) % TILE_ROWS // slots
    for chunk in range(REDUCE_CHUNKS):
        partial = jnp.zeros((rows, r_width), jnp.float32)
        for piece in range(fold):
            start = piece * width + chunk * r_width
            product = jnp.dot(hidden, w_up[:, start:start + r_width], preferred_element_type=jnp.float32)
            partial = jnp.where(row_piece == piece, product, partial)
        columns = slice(chunk * r_width, (chunk + 1) * r_width)
        send_buf[:, columns] = partial.astype(jnp.bfloat16)
        def send(k, carry):
            reduce_copy(chunk, me, peer_at(k)).start()
            return carry
        lax.fori_loop(1, peers, send, 0)
        recv_buf[my_rows, columns] = send_buf[my_rows, columns]

    for chunk in range(REDUCE_CHUNKS):
        def arrive(k, carry):
            peer = peer_at(k)
            reduce_copy(chunk, peer, peer).wait_recv()
            return carry
        lax.fori_loop(1, peers, arrive, 0)

    alike = jnp.where(id_col[:, :1] == id_row_ref[...][:1, :], 1.0, 0.0).astype(jnp.bfloat16)
    delta = jnp.dot(alike, recv_buf[...], preferred_element_type=jnp.float32)
    new_buf[section] = (current + delta).astype(jnp.bfloat16)
    for target in range(sections - 2, -1, -1):
        @pl.when(target < section)
        def _():
            new_copy(section, target).start()

    for layer in range(sections):
        @pl.when(layer > section)
        def _():
            all_new_ref[layer] = new_buf[layer]
            all_ids_ref[layer] = id_buf[layer]

        @pl.when(layer < section)
        def _():
            all_new_ref[layer] = jnp.zeros((TILE_ROWS, width), jnp.bfloat16)
            all_ids_ref[layer] = jnp.full(id_send_ref.shape, -1, jnp.int32)
    all_new_ref[section] = new_buf[section]
    all_ids_ref[section] = id_send_ref[...]
    gathered_ref[...] = gbuf[...]

    def drain(k, carry):
        peer = peer_at(k)
        for chunk in range(GATHER_CHUNKS):
            gather_copy(chunk, me, peer).wait_send()
        for chunk in range(REDUCE_CHUNKS):
            reduce_copy(chunk, me, peer).wait_send()
        return carry

    lax.fori_loop(1, peers, drain, 0)
    for target in range(sections - 1):
        @pl.when(target < section)
        def _():
            id_copy(section, target).wait_send()
            new_copy(section, target).wait_send()


def per_device(sections, peers, out_grad, x_rows, saved_u, w_up_t, w_down, gate, route_tokens, route_count):
    micro, tokens, features = out_grad.shape
    cap = gate.shape[2]
    slots = micro * cap
    fold = TILE_ROWS // slots
    width = features // fold
    hid = w_down.shape[1]
    rows = peers * TILE_ROWS

    token_ids = route_tokens[0]
    live = jnp.arange(cap)[None, :] < route_count[0]
    weights = jnp.where(live, gate[0], jnp.float32(0.0)).reshape(slots)
    base = out_grad[jnp.arange(micro)[:, None], token_ids].reshape(slots, fold, width)
    base = base.transpose(1, 0, 2).reshape(TILE_ROWS, width)
    flat_ids = (token_ids + tokens * jnp.arange(micro)[:, None]).reshape(slots)
    earlier = jnp.arange(slots)[None, :] < jnp.arange(slots)[:, None]
    repeat = jnp.any((flat_ids[:, None] == flat_ids[None, :]) & earlier, axis=1)
    piece_ids = (jnp.arange(fold)[:, None] * (micro * tokens) + flat_ids[None, :]).reshape(TILE_ROWS)
    sent_ids = jnp.where(jnp.tile(repeat, fold), -1, piece_ids)
    id_col = jnp.broadcast_to(piece_ids[:, None], (TILE_ROWS, 128))
    id_row = jnp.broadcast_to(jnp.tile(piece_ids, peers)[None, :], (8, rows))
    id_send = jnp.broadcast_to(jnp.concatenate([sent_ids, jnp.full(128 - TILE_ROWS, -1, jnp.int32)])[None, :], (8, 128))
    weight_col = jnp.broadcast_to(jnp.tile(weights, fold)[:, None], (TILE_ROWS, 128))

    pre = saved_u[0].astype(jnp.float32)
    sigmoid = jax.nn.sigmoid(pre)
    activation = (pre * sigmoid).astype(jnp.bfloat16).reshape(micro * peers * cap, hid)
    slope = sigmoid * (1.0 + pre * (1.0 - sigmoid))
    slope = slope.reshape(micro, peers, cap, hid).transpose(1, 0, 2, 3).reshape(peers, 1, slots, hid)
    slope = jnp.broadcast_to(slope, (peers, fold, slots, hid)).reshape(rows, hid)

    vmem = pl.BlockSpec(memory_space=pltpu.VMEM)
    dma = pltpu.SemaphoreType.DMA
    all_new, all_ids, gathered, hidden = pl.pallas_call(
        functools.partial(chain_kernel, (sections, peers, fold, slots)),
        out_shape=(
            jax.ShapeDtypeStruct((sections, TILE_ROWS, width), jnp.bfloat16),
            jax.ShapeDtypeStruct((sections, 8, 128), jnp.int32),
            jax.ShapeDtypeStruct((rows, width), jnp.bfloat16),
            jax.ShapeDtypeStruct((rows, hid), jnp.bfloat16),
        ),
        in_specs=[vmem] * 6 + [pl.BlockSpec(memory_space=pl.ANY)] * 2,
        out_specs=(vmem,) * 4,
        scratch_shapes=[
            pltpu.VMEM((hid, features), jnp.bfloat16),
            pltpu.VMEM((hid, features), jnp.bfloat16),
            pltpu.VMEM((rows, width), jnp.bfloat16),
            pltpu.VMEM((rows, width), jnp.bfloat16),
            pltpu.VMEM((rows, width), jnp.bfloat16),
            pltpu.VMEM((sections, TILE_ROWS, width), jnp.bfloat16),
            pltpu.VMEM((sections, 8, 128), jnp.int32),
            pltpu.VMEM((TILE_ROWS, width), jnp.bfloat16),
            dma((2,)),
            dma((GATHER_CHUNKS, peers)),
            dma((GATHER_CHUNKS, peers)),
            dma((REDUCE_CHUNKS, peers)),
            dma((REDUCE_CHUNKS, peers)),
            dma((sections,)),
            dma((sections,)),
            dma((sections,)),
            dma((sections,)),
        ],
        compiler_params=pltpu.CompilerParams(
            collective_id=0, has_side_effects=True, vmem_limit_bytes=48 * 1024 * 1024),
    )(base, weight_col, id_col, id_row, id_send, slope, w_up_t[0], w_down[0])

    hidden = hidden.reshape(peers, fold, micro, cap, hid)[:, 0].transpose(1, 0, 2, 3).reshape(-1, hid)
    scaled = gathered.reshape(peers, fold, micro, cap, width).transpose(2, 0, 3, 1, 4).reshape(-1, features)
    grad_down = jnp.einsum("rh,rd->hd", activation, scaled, preferred_element_type=jnp.float32)
    grad_up = jnp.einsum(
        "rh,rd->hd", hidden, x_rows[0].reshape(-1, features), preferred_element_type=jnp.float32)

    token = jnp.arange(micro * tokens, dtype=jnp.int32)[:, None]
    in_grad = out_grad.reshape(micro * tokens, features)
    new_rows = all_new.reshape(sections, fold, slots, width).transpose(0, 2, 1, 3).reshape(sections, slots, features)
    for layer in range(sections - 1, -1, -1):
        for slot in range(slots):
            in_grad = jnp.where(token == all_ids[layer, 0, slot], new_rows[layer, slot][None, :], in_grad)
    in_grad = in_grad.reshape(1, micro, tokens, features)
    return in_grad, grad_up.astype(jnp.bfloat16)[None], grad_down.astype(jnp.bfloat16)[None]


def solution(mesh):
    return jax.shard_map(
        functools.partial(per_device, mesh.shape["section"], mesh.shape["dp"]),
        mesh=mesh,
        in_specs=(
            P(None, "dp", None),
            P("section", None, None, None),
            P("section", None, None, "dp"),
            P("section", "dp", None),
            P("section", "dp", None),
            P("section", None, "dp"),
            P("section", None, "dp"),
            P("section", None, "dp"),
        ),
        out_specs=(
            P("section", None, "dp", None),
            P("section", "dp", None),
            P("section", "dp", None),
        ),
        check_vma=False,
    )
```

```python
import functools

import jax
import jax.numpy as jnp
from jax import lax
from jax.experimental import pallas as pl
from jax.experimental.pallas import tpu as pltpu
from jax.sharding import PartitionSpec as P

MESH = pl.DeviceIdType.MESH
TILE_ROWS = 16
CHUNKS = 3


def row_of_slot(index, peers, cap, micro):
    slot = index % (micro * cap)
    return (slot // cap) * (peers * cap) + (index // TILE_ROWS) * cap + slot % cap


def chain_kernel(
    sizes,
    token_ref, gate_ref, count_ref, grad_ref, saved_ref, w_up_hbm, w_down_hbm,
    all_new_ref, all_ids_ref, gathered_ref, hidden_ref,
    w_up, w_down, gbuf, send_buf, recv_buf, new_buf, id_buf, cur_buf, slope_buf,
    weight_sem, gather_send, gather_recv, reduce_send, reduce_recv, id_send, id_recv, new_send, new_recv,
):
    sections, peers, micro, cap = sizes
    slots = micro * cap
    fold = TILE_ROWS // slots
    section = lax.axis_index("section")
    me = lax.axis_index("dp")
    width = gbuf.shape[1]
    c_width = width // CHUNKS
    hid = w_down.shape[0]
    tokens = grad_ref.shape[1]
    span = micro * tokens
    rows = peers * TILE_ROWS

    down_copy = pltpu.make_async_copy(w_down_hbm.at[0], w_down, weight_sem.at[0])
    up_copy = pltpu.make_async_copy(w_up_hbm.at[0], w_up, weight_sem.at[1])
    down_copy.start()
    up_copy.start()

    def peer_at(k):
        return lax.rem(me + k, peers)

    barrier = pltpu.get_barrier_semaphore()

    def greet(k, carry):
        pl.semaphore_signal(barrier, inc=1, device_id=(section, peer_at(k)), device_id_type=MESH)
        return carry

    lax.fori_loop(1, peers, greet, 0)
    for k in range(1, sections):
        other = lax.rem(section + k, sections)
        pl.semaphore_signal(barrier, inc=1, device_id=(other, me), device_id_type=MESH)

    flat, weight = [], []
    for m in range(micro):
        for c in range(cap):
            flat.append(token_ref[0, m, c] + m * tokens)
            weight.append(jnp.where(c < count_ref[0, m, 0], gate_ref[0, m, c], jnp.float32(0.0)))
    sent = []
    for k in range(slots):
        mine = flat[k]
        for e in range(k):
            mine = jnp.where(flat[e] == flat[k], -sections * TILE_ROWS * span, mine)
        sent.append(mine)

    def spread(values, slot, start):
        out = start
        for k in range(slots):
            out = jnp.where(slot == k, values[k], out)
        return out

    row = lax.broadcasted_iota(jnp.int32, (TILE_ROWS, 128), 0)
    lane = lax.broadcasted_iota(jnp.int32, (8, 128), 1)
    lane_all = lax.broadcasted_iota(jnp.int32, (8, rows), 1) % TILE_ROWS
    id_col = spread(flat, row % slots, jnp.zeros((TILE_ROWS, 128), jnp.int32)) + row // slots * span
    weight_col = spread(weight, row % slots, jnp.zeros((TILE_ROWS, 128), jnp.float32))
    id_row = spread(flat, lane_all % slots, jnp.zeros((8, rows), jnp.int32)) + lane_all // slots * span
    sent_row = spread(sent, lane % slots, jnp.zeros((8, 128), jnp.int32)) + lane // slots * span
    id_buf[section] = jnp.where((lane < TILE_ROWS) & (sent_row >= 0), sent_row, -1)

    flat_col = id_col[:, :1] % span
    piece_col = lax.broadcasted_iota(jnp.int32, (TILE_ROWS, span), 0) // slots
    token_lane = lax.broadcasted_iota(jnp.int32, (TILE_ROWS, span), 1)
    base = jnp.zeros((TILE_ROWS, width), jnp.float32)
    for piece in range(fold):
        pick = jnp.where((token_lane == flat_col) & (piece_col == piece), 1.0, 0.0).astype(jnp.bfloat16)
        part = grad_ref[:, :, piece * width:(piece + 1) * width].reshape(span, width)
        base = base + jnp.dot(pick, part, preferred_element_type=jnp.float32)
    cur_buf[...] = base

    source = row_of_slot(lax.broadcasted_iota(jnp.int32, (rows, slots * peers), 0), peers, cap, micro)
    order = jnp.where(source == lax.broadcasted_iota(jnp.int32, (rows, slots * peers), 1), 1.0, 0.0)
    pre = jnp.dot(order.astype(jnp.bfloat16), saved_ref[0].reshape(slots * peers, hid), preferred_element_type=jnp.float32)
    sigmoid = jax.nn.sigmoid(pre)
    slope_buf[...] = sigmoid * (1.0 + pre * (1.0 - sigmoid))

    pl.semaphore_wait(barrier, peers - 1 + sections - 1)

    def id_copy(source, target):
        return pltpu.make_async_remote_copy(
            src_ref=id_buf.at[source], dst_ref=id_buf.at[source],
            send_sem=id_send.at[target], recv_sem=id_recv.at[source],
            device_id=(target, me), device_id_type=MESH)

    def columns_of(chunk):
        return pl.ds(chunk * c_width, c_width)

    def rows_of(peer):
        return pl.ds(pl.multiple_of(peer * TILE_ROWS, TILE_ROWS), TILE_ROWS)

    def new_copy(chunk, source, target):
        place = new_buf.at[source, :, columns_of(chunk)]
        return pltpu.make_async_remote_copy(
            src_ref=place, dst_ref=place,
            send_sem=new_send.at[chunk, target], recv_sem=new_recv.at[chunk, source],
            device_id=(target, me), device_id_type=MESH)

    def gather_copy(chunk, source, target):
        place = gbuf.at[rows_of(source), columns_of(chunk)]
        return pltpu.make_async_remote_copy(
            src_ref=place, dst_ref=place,
            send_sem=gather_send.at[chunk, target], recv_sem=gather_recv.at[chunk, source],
            device_id=(section, target), device_id_type=MESH)

    def reduce_copy(chunk, source, target):
        return pltpu.make_async_remote_copy(
            src_ref=send_buf.at[rows_of(target), columns_of(chunk)],
            dst_ref=recv_buf.at[rows_of(source), columns_of(chunk)],
            send_sem=reduce_send.at[chunk, target], recv_sem=reduce_recv.at[chunk, source],
            device_id=(section, target), device_id_type=MESH)

    for target in range(sections - 1):
        @pl.when(target < section)
        def _():
            id_copy(section, target).start()

    def take_newer(upper, columns):
        picks = jnp.where(id_col[:, :TILE_ROWS] == id_buf[upper][:1, :TILE_ROWS], 1.0, 0.0)
        hit = jnp.max(picks, axis=1, keepdims=True) > 0.5
        taken = jnp.dot(picks.astype(jnp.bfloat16), new_buf[upper, :, columns], preferred_element_type=jnp.float32)
        cur_buf[:, columns] = jnp.where(hit, taken, cur_buf[:, columns])

    for upper in range(sections - 1, 1, -1):
        @pl.when(upper > section + 1)
        def _():
            id_copy(upper, upper).wait_recv()
            for chunk in range(CHUNKS):
                new_copy(chunk, upper, upper).wait_recv()
            take_newer(upper, slice(0, width))

    above = lax.rem(section + 1, sections)
    has_above = section < sections - 1

    @pl.when(has_above)
    def _():
        id_copy(above, above).wait_recv()

    my_rows = rows_of(me)
    for chunk in range(CHUNKS):
        columns = slice(chunk * c_width, (chunk + 1) * c_width)

        @pl.when(has_above)
        def _():
            new_copy(chunk, above, above).wait_recv()
            take_newer(above, columns)

        gbuf[my_rows, columns] = (weight_col[:, :1] * cur_buf[:, columns]).astype(jnp.bfloat16)

        def send(k, carry):
            gather_copy(chunk, me, peer_at(k)).start()
            return carry

        lax.fori_loop(1, peers, send, 0)

    down_copy.wait()
    row_piece = lax.broadcasted_iota(jnp.int32, (rows, c_width), 0) % TILE_ROWS // slots
    keep = [jnp.where(row_piece == piece, 1.0, 0.0).astype(jnp.bfloat16) for piece in range(fold)]
    total = jnp.zeros((hid, rows), jnp.float32)
    for chunk in range(CHUNKS):
        def arrive(k, carry):
            peer = peer_at(k)
            gather_copy(chunk, peer, peer).wait_recv()
            return carry

        lax.fori_loop(1, peers, arrive, 0)
        block = gbuf[:, chunk * c_width:(chunk + 1) * c_width]
        starts = [piece * width + chunk * c_width for piece in range(fold)]
        left = jnp.concatenate([w_down[:, start:start + c_width] for start in starts], axis=1)
        right = jnp.concatenate([block * keep[piece] for piece in range(fold)], axis=1)
        total = total + lax.dot_general(
            left, right, (((1,), (1,)), ((), ())), preferred_element_type=jnp.float32)

    back = total.T.reshape(peers, TILE_ROWS, hid)
    summed = back
    for k in range(1, fold):
        cut = k * slots
        summed = summed + jnp.concatenate([back[:, cut:], back[:, :cut]], axis=1)
    hidden = (summed.reshape(rows, hid) * slope_buf[...]).astype(jnp.bfloat16)

    up_copy.wait()
    for chunk in range(CHUNKS):
        partial = jnp.zeros((rows, c_width), jnp.float32)
        for piece in range(fold):
            start = piece * width + chunk * c_width
            product = jnp.dot(hidden, w_up[:, start:start + c_width], preferred_element_type=jnp.float32)
            partial = jnp.where(row_piece == piece, product, partial)
        columns = slice(chunk * c_width, (chunk + 1) * c_width)
        send_buf[:, columns] = partial.astype(jnp.bfloat16)

        def send(k, carry):
            reduce_copy(chunk, me, peer_at(k)).start()
            return carry

        lax.fori_loop(1, peers, send, 0)
        recv_buf[my_rows, columns] = send_buf[my_rows, columns]

    hidden_ref[...] = hidden
    gathered_ref[...] = gbuf[...]
    for layer in range(sections):
        @pl.when(layer > section)
        def _():
            all_new_ref[layer] = new_buf[layer]
            all_ids_ref[layer] = id_buf[layer]

        @pl.when(layer < section)
        def _():
            all_new_ref[layer] = jnp.zeros((TILE_ROWS, width), jnp.bfloat16)
            all_ids_ref[layer] = jnp.full((8, 128), -1, jnp.int32)
    all_ids_ref[section] = id_buf[section]

    alike = jnp.where(id_col[:, :1] == id_row[:1, :], 1.0, 0.0).astype(jnp.bfloat16)
    for chunk in range(CHUNKS):
        def arrive(k, carry):
            peer = peer_at(k)
            reduce_copy(chunk, peer, peer).wait_recv()
            return carry

        lax.fori_loop(1, peers, arrive, 0)
        columns = slice(chunk * c_width, (chunk + 1) * c_width)
        delta = jnp.dot(alike, recv_buf[:, columns], preferred_element_type=jnp.float32)
        new_buf[section, :, columns] = (cur_buf[:, columns] + delta).astype(jnp.bfloat16)

        @pl.when(section > 0)
        def _():
            new_copy(chunk, section, section - 1).start()

    for target in range(sections - 2):
        @pl.when(target < section - 1)
        def _():
            for chunk in range(CHUNKS):
                new_copy(chunk, section, target).start()
    all_new_ref[section] = new_buf[section]

    def drain(k, carry):
        peer = peer_at(k)
        for chunk in range(CHUNKS):
            gather_copy(chunk, me, peer).wait_send()
            reduce_copy(chunk, me, peer).wait_send()
        return carry

    lax.fori_loop(1, peers, drain, 0)
    for target in range(sections - 1):
        @pl.when(target < section)
        def _():
            id_copy(section, target).wait_send()
            for chunk in range(CHUNKS):
                new_copy(chunk, section, target).wait_send()


def gradient_kernel(
    sizes,
    hidden_ref, gathered_ref, saved_ref, x_ref, grad_ref, new_ref, id_ref,
    in_grad_ref, grad_up_ref, grad_down_ref,
    hidden_t, activation_t, picks, order_buf,
):
    sections, peers, micro, cap, per_piece = sizes
    slots = micro * cap
    step = pl.program_id(0)
    piece = step // per_piece
    hid = hidden_t.shape[0]
    all_slots = peers * slots
    rows = peers * TILE_ROWS
    span = grad_ref.shape[0] * grad_ref.shape[1]
    index = lax.broadcasted_iota(jnp.int32, (all_slots, rows), 1)

    @pl.when(step == 0)
    def _():
        place = row_of_slot(index, peers, cap, micro)
        order = jnp.where(place == lax.broadcasted_iota(jnp.int32, (all_slots, rows), 0), 1.0, 0.0)
        order_buf[...] = order
        first = jnp.where(index % TILE_ROWS < slots, order, 0.0).astype(jnp.bfloat16)
        hidden = jnp.dot(first, hidden_ref[...], preferred_element_type=jnp.float32)
        hidden_t[...] = hidden.T.astype(jnp.bfloat16)
        pre = saved_ref[0].reshape(all_slots, hid).astype(jnp.float32)
        activation_t[...] = (pre * jax.nn.sigmoid(pre)).T.astype(jnp.bfloat16)
        token = lax.broadcasted_iota(jnp.int32, (span, TILE_ROWS), 0)
        found = jnp.zeros((span, 1), jnp.float32)
        for layer in range(sections):
            ids = id_ref[layer][:1, :TILE_ROWS]
            same = jnp.where((token == ids % span) & (ids >= 0), 1.0, 0.0) * (1.0 - found)
            picks[:, layer * TILE_ROWS:(layer + 1) * TILE_ROWS] = same
            found = jnp.maximum(found, jnp.max(same, axis=1, keepdims=True))

    width = x_ref.shape[3]
    mine = jnp.where(index % TILE_ROWS // slots == piece, order_buf[...], 0.0).astype(jnp.bfloat16)
    scaled = jnp.dot(mine, gathered_ref[...], preferred_element_type=jnp.float32).astype(jnp.bfloat16)
    grad_down_ref[0] = jnp.dot(
        activation_t[...], scaled, preferred_element_type=jnp.float32).astype(jnp.bfloat16)
    grad_up_ref[0] = jnp.dot(
        hidden_t[...], x_ref[0].reshape(all_slots, width), preferred_element_type=jnp.float32).astype(jnp.bfloat16)

    lane = lax.broadcasted_iota(jnp.int32, picks.shape, 1)
    chosen = jnp.where(lane % TILE_ROWS // slots == piece, picks[...], 0.0)
    hit = jnp.max(chosen, axis=1, keepdims=True) > 0.5
    newest = jnp.dot(
        chosen.astype(jnp.bfloat16), new_ref[...].reshape(sections * TILE_ROWS, width),
        preferred_element_type=jnp.float32)
    old = grad_ref[...].reshape(span, width).astype(jnp.float32)
    in_grad_ref[0] = jnp.where(hit, newest, old).astype(jnp.bfloat16).reshape(grad_ref.shape)


def per_device(sections, peers, out_grad, x_rows, saved_u, w_up_t, w_down, gate, route_tokens, route_count):
    micro, tokens, features = out_grad.shape
    cap = gate.shape[2]
    slots = micro * cap
    fold = TILE_ROWS // slots
    width = features // fold
    hid = w_down.shape[1]
    rows = peers * TILE_ROWS
    sizes = (sections, peers, micro, cap)

    vmem = pl.BlockSpec(memory_space=pltpu.VMEM)
    smem = pl.BlockSpec(memory_space=pltpu.SMEM)
    hbm = pl.BlockSpec(memory_space=pl.ANY)
    dma = pltpu.SemaphoreType.DMA
    all_new, all_ids, gathered, hidden = pl.pallas_call(
        functools.partial(chain_kernel, sizes),
        out_shape=(
            jax.ShapeDtypeStruct((sections, TILE_ROWS, width), jnp.bfloat16),
            jax.ShapeDtypeStruct((sections, 8, 128), jnp.int32),
            jax.ShapeDtypeStruct((rows, width), jnp.bfloat16),
            jax.ShapeDtypeStruct((rows, hid), jnp.bfloat16),
        ),
        in_specs=[smem, smem, smem, vmem, vmem, hbm, hbm],
        out_specs=(vmem,) * 4,
        scratch_shapes=[
            pltpu.VMEM((hid, features), jnp.bfloat16),
            pltpu.VMEM((hid, features), jnp.bfloat16),
            pltpu.VMEM((rows, width), jnp.bfloat16),
            pltpu.VMEM((rows, width), jnp.bfloat16),
            pltpu.VMEM((rows, width), jnp.bfloat16),
            pltpu.VMEM((sections, TILE_ROWS, width), jnp.bfloat16),
            pltpu.VMEM((sections, 8, 128), jnp.int32),
            pltpu.VMEM((TILE_ROWS, width), jnp.float32),
            pltpu.VMEM((rows, hid), jnp.float32),
            dma((2,)),
            dma((CHUNKS, peers)),
            dma((CHUNKS, peers)),
            dma((CHUNKS, peers)),
            dma((CHUNKS, peers)),
            dma((sections,)),
            dma((sections,)),
            dma((CHUNKS, sections)),
            dma((CHUNKS, sections)),
        ],
        compiler_params=pltpu.CompilerParams(
            collective_id=0, has_side_effects=True, vmem_limit_bytes=48 * 1024 * 1024),
    )(route_tokens, gate, route_count, out_grad, saved_u, w_up_t, w_down)

    per_piece = CHUNKS
    block = width // per_piece
    slot_rows = peers * cap
    return pl.pallas_call(
        functools.partial(gradient_kernel, sizes + (per_piece,)),
        grid=(fold * per_piece,),
        out_shape=(
            jax.ShapeDtypeStruct((1, micro, tokens, features), jnp.bfloat16),
            jax.ShapeDtypeStruct((1, hid, features), jnp.bfloat16),
            jax.ShapeDtypeStruct((1, hid, features), jnp.bfloat16),
        ),
        in_specs=[
            pl.BlockSpec((rows, hid), lambda i: (0, 0)),
            pl.BlockSpec((rows, block), lambda i: (0, i % per_piece)),
            pl.BlockSpec((1, micro, slot_rows, hid), lambda i: (0, 0, 0, 0)),
            pl.BlockSpec((1, micro, slot_rows, block), lambda i: (0, 0, 0, i)),
            pl.BlockSpec((micro, tokens, block), lambda i: (0, 0, i)),
            pl.BlockSpec((sections, TILE_ROWS, block), lambda i: (0, 0, i % per_piece)),
            pl.BlockSpec((sections, 8, 128), lambda i: (0, 0, 0)),
        ],
        out_specs=(
            pl.BlockSpec((1, micro, tokens, block), lambda i: (0, 0, 0, i)),
            pl.BlockSpec((1, hid, block), lambda i: (0, 0, i)),
            pl.BlockSpec((1, hid, block), lambda i: (0, 0, i)),
        ),
        scratch_shapes=[
            pltpu.VMEM((hid, peers * slots), jnp.bfloat16),
            pltpu.VMEM((hid, peers * slots), jnp.bfloat16),
            pltpu.VMEM((micro * tokens, sections * TILE_ROWS), jnp.float32),
            pltpu.VMEM((peers * slots, rows), jnp.float32),
        ],
        compiler_params=pltpu.CompilerParams(vmem_limit_bytes=32 * 1024 * 1024),
    )(hidden, gathered, saved_u, x_rows, out_grad, all_new, all_ids)


def solution(mesh):
    return jax.shard_map(
        functools.partial(per_device, mesh.shape["section"], mesh.shape["dp"]),
        mesh=mesh,
        in_specs=(
            P(None, "dp", None),
            P("section", None, None, None),
            P("section", None, None, "dp"),
            P("section", "dp", None),
            P("section", "dp", None),
            P("section", None, "dp"),
            P("section", None, "dp"),
            P("section", None, "dp"),
        ),
        out_specs=(
            P("section", None, "dp", None),
            P("section", "dp", None),
            P("section", "dp", None),
        ),
        check_vma=False,
    )
```

```python
import functools

import jax
import jax.numpy as jnp
from jax import lax
from jax.experimental import pallas as pl
from jax.experimental.pallas import tpu as pltpu
from jax.sharding import PartitionSpec as P

MESH = pl.DeviceIdType.MESH
TILE_ROWS = 16
CHUNKS = 3


def row_of_slot(index, peers, cap, micro):
    slot = index % (micro * cap)
    block = index // TILE_ROWS
    peer = block % (peers // 2) * 2 + block // (peers // 2)
    return (slot // cap) * (peers * cap) + peer * cap + slot % cap


def chain_kernel(
    sizes,
    token_hbm, gate_hbm, count_hbm, grad_hbm, saved_hbm, w_up_hbm, w_down_hbm,
    all_new_ref, picks_ref, scaled_ref, hidden_t_ref, activation_t_ref,
    token_ref, gate_ref, count_ref, grad_ref, saved_ref,
    w_up, w_down, gbuf, send_buf, pair_buf, sum_buf, recv_buf, new_buf, id_buf, cur_buf, slope_buf,
    load_sem, gather_send, gather_recv, share_send, share_recv, pair_send, pair_recv,
    reduce_send, reduce_recv, id_send, id_recv, new_send, new_recv,
):
    sections, peers, micro, cap = sizes
    slots = micro * cap
    fold = TILE_ROWS // slots
    section = lax.axis_index("section")
    me = lax.axis_index("dp")
    width = gbuf.shape[1]
    c_width = width // CHUNKS
    hid = w_down.shape[0]
    tokens = grad_ref.shape[1]
    span = micro * tokens
    rows = peers * TILE_ROWS
    chips = peers // 2
    half = chips * TILE_ROWS
    core = lax.rem(me, 2)
    chip = me // 2
    sibling = me + 1 - 2 * core

    small = [
        pltpu.make_async_copy(source, target, load_sem.at[2 + k])
        for k, (source, target) in enumerate((
            (token_hbm, token_ref), (gate_hbm, gate_ref), (count_hbm, count_ref),
            (grad_hbm, grad_ref), (saved_hbm, saved_ref)))
    ]
    for copy in small:
        copy.start()
    down_copy = pltpu.make_async_copy(w_down_hbm.at[0], w_down, load_sem.at[0])
    up_copy = pltpu.make_async_copy(w_up_hbm.at[0], w_up, load_sem.at[1])
    down_copy.start()

    def chip_at(k):
        return lax.rem(chip + k, chips)

    barrier = pltpu.get_barrier_semaphore()

    def greet(k, carry):
        pl.semaphore_signal(barrier, inc=1, device_id=(section, chip_at(k) * 2 + core), device_id_type=MESH)
        return carry

    lax.fori_loop(1, chips, greet, 0)
    pl.semaphore_signal(barrier, inc=1, device_id=(section, sibling), device_id_type=MESH)
    for k in range(1, sections):
        other = lax.rem(section + k, sections)
        pl.semaphore_signal(barrier, inc=1, device_id=(other, me), device_id_type=MESH)

    for copy in small:
        copy.wait()

    flat, weight = [], []
    for m in range(micro):
        for c in range(cap):
            flat.append(token_ref[0, m, c] + m * tokens)
            weight.append(jnp.where(c < count_ref[0, m, 0], gate_ref[0, m, c], jnp.float32(0.0)))
    sent = []
    for k in range(slots):
        mine = flat[k]
        for e in range(k):
            mine = jnp.where(flat[e] == flat[k], -sections * TILE_ROWS * span, mine)
        sent.append(mine)

    def spread(values, slot, start):
        out = start
        for k in range(slots):
            out = jnp.where(slot == k, values[k], out)
        return out

    row = lax.broadcasted_iota(jnp.int32, (TILE_ROWS, 128), 0)
    lane = lax.broadcasted_iota(jnp.int32, (8, 128), 1)
    lane_all = lax.broadcasted_iota(jnp.int32, (8, half), 1) % TILE_ROWS
    id_col = spread(flat, row % slots, jnp.zeros((TILE_ROWS, 128), jnp.int32)) + row // slots * span
    weight_col = spread(weight, row % slots, jnp.zeros((TILE_ROWS, 128), jnp.float32))
    id_row = spread(flat, lane_all % slots, jnp.zeros((8, half), jnp.int32)) + lane_all // slots * span
    sent_row = spread(sent, lane % slots, jnp.zeros((8, 128), jnp.int32)) + lane // slots * span
    id_buf[section] = jnp.where((lane < TILE_ROWS) & (sent_row >= 0), sent_row, -1)

    flat_col = id_col[:, :1] % span
    piece_col = lax.broadcasted_iota(jnp.int32, (TILE_ROWS, span), 0) // slots
    token_lane = lax.broadcasted_iota(jnp.int32, (TILE_ROWS, span), 1)
    base = jnp.zeros((TILE_ROWS, width), jnp.float32)
    for piece in range(fold):
        pick = jnp.where((token_lane == flat_col) & (piece_col == piece), 1.0, 0.0).astype(jnp.bfloat16)
        part = grad_ref[:, :, piece * width:(piece + 1) * width].reshape(span, width)
        base = base + jnp.dot(pick, part, preferred_element_type=jnp.float32)
    cur_buf[...] = base

    pl.semaphore_wait(barrier, chips + sections - 1)

    def id_copy(source, target):
        return pltpu.make_async_remote_copy(
            src_ref=id_buf.at[source], dst_ref=id_buf.at[source],
            send_sem=id_send.at[target], recv_sem=id_recv.at[source],
            device_id=(target, me), device_id_type=MESH)

    def columns_of(chunk):
        return pl.ds(chunk * c_width, c_width)

    def rows_of(peer):
        return pl.ds(pl.multiple_of(peer * TILE_ROWS, TILE_ROWS), TILE_ROWS)

    def new_copy(chunk, source, target):
        place = new_buf.at[source, :, columns_of(chunk)]
        return pltpu.make_async_remote_copy(
            src_ref=place, dst_ref=place,
            send_sem=new_send.at[chunk, target], recv_sem=new_recv.at[chunk, source],
            device_id=(target, me), device_id_type=MESH)

    def block_of(a_chip, a_core):
        return pl.ds(pl.multiple_of(a_core * half + a_chip * TILE_ROWS, TILE_ROWS), TILE_ROWS)

    def half_of(a_core):
        return pl.ds(pl.multiple_of(a_core * half, TILE_ROWS), half)

    def gather_copy(chunk, source, target):
        place = gbuf.at[block_of(source, core), columns_of(chunk)]
        return pltpu.make_async_remote_copy(
            src_ref=place, dst_ref=place,
            send_sem=gather_send.at[chunk, target], recv_sem=gather_recv.at[chunk, source],
            device_id=(section, target * 2 + core), device_id_type=MESH)

    def share_copy(chunk, a_core):
        place = gbuf.at[half_of(a_core), columns_of(chunk)]
        return pltpu.make_async_remote_copy(
            src_ref=place, dst_ref=place,
            send_sem=share_send.at[chunk], recv_sem=share_recv.at[chunk],
            device_id=(section, sibling), device_id_type=MESH)

    def pair_copy(chunk):
        return pltpu.make_async_remote_copy(
            src_ref=send_buf.at[half_of(1 - core), columns_of(chunk)],
            dst_ref=pair_buf.at[:, columns_of(chunk)],
            send_sem=pair_send.at[chunk], recv_sem=pair_recv.at[chunk],
            device_id=(section, sibling), device_id_type=MESH)

    def reduce_copy(chunk, source, target):
        return pltpu.make_async_remote_copy(
            src_ref=sum_buf.at[rows_of(target), columns_of(chunk)],
            dst_ref=recv_buf.at[rows_of(source), columns_of(chunk)],
            send_sem=reduce_send.at[chunk, target], recv_sem=reduce_recv.at[chunk, source],
            device_id=(section, target * 2 + core), device_id_type=MESH)

    for target in range(sections - 1):
        @pl.when(target < section)
        def _():
            id_copy(section, target).start()

    def take_newer(upper, columns):
        picks = jnp.where(id_col[:, :TILE_ROWS] == id_buf[upper][:1, :TILE_ROWS], 1.0, 0.0)
        hit = jnp.max(picks, axis=1, keepdims=True) > 0.5
        taken = jnp.dot(picks.astype(jnp.bfloat16), new_buf[upper, :, columns], preferred_element_type=jnp.float32)
        cur_buf[:, columns] = jnp.where(hit, taken, cur_buf[:, columns])

    for upper in range(sections - 1, 1, -1):
        @pl.when(upper > section + 1)
        def _():
            id_copy(upper, upper).wait_recv()
            for chunk in range(CHUNKS):
                new_copy(chunk, upper, upper).wait_recv()
            take_newer(upper, slice(0, width))

    above = lax.rem(section + 1, sections)
    has_above = section < sections - 1

    def prepare():
        for layer in range(sections):
            @pl.when(layer < section)
            def _():
                all_new_ref[layer] = jnp.zeros((TILE_ROWS, width), jnp.bfloat16)
                id_buf[layer] = jnp.full((8, 128), -1, jnp.int32)
        pre = saved_ref[0].reshape(slots * peers, hid).astype(jnp.float32)
        activation_t_ref[...] = (pre * jax.nn.sigmoid(pre)).T.astype(jnp.bfloat16)
        token = lax.broadcasted_iota(jnp.int32, (span, TILE_ROWS), 0)
        found = jnp.zeros((span, 1), jnp.float32)
        for layer in range(sections):
            ids = id_buf[layer][:1, :TILE_ROWS]
            same = jnp.where((token == ids % span) & (ids >= 0), 1.0, 0.0) * (1.0 - found)
            picks_ref[:, layer * TILE_ROWS:(layer + 1) * TILE_ROWS] = same
            found = jnp.maximum(found, jnp.max(same, axis=1, keepdims=True))

    @pl.when(has_above)
    def _():
        id_copy(above, above).wait_recv()
        prepare()

    my_rows = block_of(chip, core)
    for chunk in range(CHUNKS):
        columns = slice(chunk * c_width, (chunk + 1) * c_width)

        @pl.when(has_above)
        def _():
            new_copy(chunk, above, above).wait_recv()
            take_newer(above, columns)

        gbuf[my_rows, columns] = (weight_col[:, :1] * cur_buf[:, columns]).astype(jnp.bfloat16)

        def send(k, carry):
            gather_copy(chunk, chip, chip_at(k)).start()
            return carry

        lax.fori_loop(1, chips, send, 0)

    source = row_of_slot(lax.broadcasted_iota(jnp.int32, (rows, slots * peers), 0), peers, cap, micro)
    order = jnp.where(source == lax.broadcasted_iota(jnp.int32, (rows, slots * peers), 1), 1.0, 0.0)
    pre = jnp.dot(order.astype(jnp.bfloat16), saved_ref[0].reshape(slots * peers, hid), preferred_element_type=jnp.float32)
    sigmoid = jax.nn.sigmoid(pre)
    slope_buf[...] = sigmoid * (1.0 + pre * (1.0 - sigmoid))

    down_copy.wait()
    up_copy.start()
    row_piece = lax.broadcasted_iota(jnp.int32, (rows, c_width), 0) % TILE_ROWS // slots
    keep = [jnp.where(row_piece == piece, 1.0, 0.0).astype(jnp.bfloat16) for piece in range(fold)]
    total = jnp.zeros((hid, rows), jnp.float32)
    def pass_on(chunk):
        def arrive(k, carry):
            other = chip_at(k)
            gather_copy(chunk, other, other).wait_recv()
            return carry

        lax.fori_loop(1, chips, arrive, 0)
        share_copy(chunk, core).start()

    pass_on(0)
    for chunk in range(CHUNKS):
        if chunk + 1 < CHUNKS:
            pass_on(chunk + 1)
        share_copy(chunk, 1 - core).wait_recv()
        block = gbuf[:, chunk * c_width:(chunk + 1) * c_width]
        starts = [piece * width + chunk * c_width for piece in range(fold)]
        left = jnp.concatenate([w_down[:, start:start + c_width] for start in starts], axis=1)
        right = jnp.concatenate([block * keep[piece] for piece in range(fold)], axis=1)
        total = total + lax.dot_general(
            left, right, (((1,), (1,)), ((), ())), preferred_element_type=jnp.float32)

    back = total.T.reshape(peers, TILE_ROWS, hid)
    summed = back
    for k in range(1, fold):
        cut = k * slots
        summed = summed + jnp.concatenate([back[:, cut:], back[:, :cut]], axis=1)
    hidden = (summed.reshape(rows, hid) * slope_buf[...]).astype(jnp.bfloat16)

    def send_sums(chunk):
        columns = slice(chunk * c_width, (chunk + 1) * c_width)
        pair_copy(chunk).wait_recv()
        both = send_buf[half_of(core), columns].astype(jnp.float32) + pair_buf[:, columns].astype(jnp.float32)
        sum_buf[:, columns] = both.astype(jnp.bfloat16)

        def send(k, carry):
            reduce_copy(chunk, chip, chip_at(k)).start()
            return carry

        lax.fori_loop(1, chips, send, 0)
        recv_buf[rows_of(chip), columns] = sum_buf[rows_of(chip), columns]

    up_copy.wait()
    for chunk in range(CHUNKS):
        partial = jnp.zeros((rows, c_width), jnp.float32)
        for piece in range(fold):
            start = piece * width + chunk * c_width
            product = jnp.dot(hidden, w_up[:, start:start + c_width], preferred_element_type=jnp.float32)
            partial = jnp.where(row_piece == piece, product, partial)
        columns = slice(chunk * c_width, (chunk + 1) * c_width)
        send_buf[:, columns] = partial.astype(jnp.bfloat16)

        pair_copy(chunk).start()
        if chunk > 0:
            send_sums(chunk - 1)
    send_sums(CHUNKS - 1)

    source = row_of_slot(lax.broadcasted_iota(jnp.int32, (slots * peers, rows), 1), peers, cap, micro)
    order = jnp.where(source == lax.broadcasted_iota(jnp.int32, (slots * peers, rows), 0), 1.0, 0.0)
    piece_lane = lax.broadcasted_iota(jnp.int32, (slots * peers, rows), 1) % TILE_ROWS // slots
    for piece in range(fold):
        mine = jnp.where(piece_lane == piece, order, 0.0).astype(jnp.bfloat16)
        if piece == 0:
            hidden_t_ref[...] = jnp.dot(mine, hidden, preferred_element_type=jnp.float32).T.astype(jnp.bfloat16)
        scaled_ref[:, piece * width:(piece + 1) * width] = jnp.dot(
            mine, gbuf[...], preferred_element_type=jnp.float32).astype(jnp.bfloat16)
    for layer in range(sections):
        @pl.when(layer > section)
        def _():
            all_new_ref[layer] = new_buf[layer]

    alike = jnp.where(id_col[:, :1] == id_row[:1, :], 1.0, 0.0).astype(jnp.bfloat16)
    for chunk in range(CHUNKS):
        def arrive(k, carry):
            other = chip_at(k)
            reduce_copy(chunk, other, other).wait_recv()
            return carry

        lax.fori_loop(1, chips, arrive, 0)
        columns = slice(chunk * c_width, (chunk + 1) * c_width)
        delta = jnp.dot(alike, recv_buf[:, columns], preferred_element_type=jnp.float32)
        new_buf[section, :, columns] = (cur_buf[:, columns] + delta).astype(jnp.bfloat16)

        @pl.when(section > 0)
        def _():
            new_copy(chunk, section, section - 1).start()

    for target in range(sections - 2):
        @pl.when(target < section - 1)
        def _():
            for chunk in range(CHUNKS):
                new_copy(chunk, section, target).start()
    all_new_ref[section] = new_buf[section]

    @pl.when(jnp.logical_not(has_above))
    def _():
        prepare()

    def drain(k, carry):
        other = chip_at(k)
        for chunk in range(CHUNKS):
            gather_copy(chunk, chip, other).wait_send()
            reduce_copy(chunk, chip, other).wait_send()
        return carry

    lax.fori_loop(1, chips, drain, 0)
    for chunk in range(CHUNKS):
        share_copy(chunk, core).wait_send()
        pair_copy(chunk).wait_send()
    for target in range(sections - 1):
        @pl.when(target < section)
        def _():
            id_copy(section, target).wait_send()
            for chunk in range(CHUNKS):
                new_copy(chunk, section, target).wait_send()


def gradient_kernel(
    sizes,
    hidden_t_ref, activation_t_ref, scaled_ref, x_ref, grad_ref, new_ref, picks_ref,
    in_grad_ref, grad_up_ref, grad_down_ref,
):
    sections, slots, per_piece = sizes
    piece = pl.program_id(0) // per_piece
    span = grad_ref.shape[0] * grad_ref.shape[1]
    width = x_ref.shape[3]
    grad_down_ref[0] = jnp.dot(
        activation_t_ref[...], scaled_ref[...], preferred_element_type=jnp.float32).astype(jnp.bfloat16)
    grad_up_ref[0] = jnp.dot(
        hidden_t_ref[...], x_ref[0].reshape(-1, width), preferred_element_type=jnp.float32).astype(jnp.bfloat16)

    lane = lax.broadcasted_iota(jnp.int32, picks_ref.shape, 1)
    chosen = jnp.where(lane % TILE_ROWS // slots == piece, picks_ref[...], 0.0)
    hit = jnp.max(chosen, axis=1, keepdims=True) > 0.5
    newest = jnp.dot(
        chosen.astype(jnp.bfloat16), new_ref[...].reshape(sections * TILE_ROWS, width),
        preferred_element_type=jnp.float32)
    old = grad_ref[...].reshape(span, width).astype(jnp.float32)
    in_grad_ref[0] = jnp.where(hit, newest, old).astype(jnp.bfloat16).reshape(grad_ref.shape)


def per_device(sections, peers, out_grad, x_rows, saved_u, w_up_t, w_down, gate, route_tokens, route_count):
    micro, tokens, features = out_grad.shape
    cap = gate.shape[2]
    slots = micro * cap
    fold = TILE_ROWS // slots
    width = features // fold
    hid = w_down.shape[1]
    rows = peers * TILE_ROWS
    sizes = (sections, peers, micro, cap)

    vmem = pl.BlockSpec(memory_space=pltpu.VMEM)
    hbm = pl.BlockSpec(memory_space=pl.ANY)
    dma = pltpu.SemaphoreType.DMA
    half = rows // 2
    chips = peers // 2
    all_rows = peers * slots
    all_new, picks, scaled, hidden_t, activation_t = pl.pallas_call(
        functools.partial(chain_kernel, sizes),
        out_shape=(
            jax.ShapeDtypeStruct((sections, TILE_ROWS, width), jnp.bfloat16),
            jax.ShapeDtypeStruct((micro * tokens, sections * TILE_ROWS), jnp.float32),
            jax.ShapeDtypeStruct((all_rows, features), jnp.bfloat16),
            jax.ShapeDtypeStruct((hid, all_rows), jnp.bfloat16),
            jax.ShapeDtypeStruct((hid, all_rows), jnp.bfloat16),
        ),
        in_specs=[hbm] * 7,
        out_specs=(vmem,) * 5,
        scratch_shapes=[
            pltpu.SMEM(route_tokens.shape, jnp.int32),
            pltpu.SMEM(gate.shape, jnp.float32),
            pltpu.SMEM(route_count.shape, jnp.int32),
            pltpu.VMEM(out_grad.shape, jnp.bfloat16),
            pltpu.VMEM(saved_u.shape, jnp.bfloat16),
            pltpu.VMEM((hid, features), jnp.bfloat16),
            pltpu.VMEM((hid, features), jnp.bfloat16),
            pltpu.VMEM((rows, width), jnp.bfloat16),
            pltpu.VMEM((rows, width), jnp.bfloat16),
            pltpu.VMEM((half, width), jnp.bfloat16),
            pltpu.VMEM((half, width), jnp.bfloat16),
            pltpu.VMEM((half, width), jnp.bfloat16),
            pltpu.VMEM((sections, TILE_ROWS, width), jnp.bfloat16),
            pltpu.VMEM((sections, 8, 128), jnp.int32),
            pltpu.VMEM((TILE_ROWS, width), jnp.float32),
            pltpu.VMEM((rows, hid), jnp.float32),
            dma((7,)),
            dma((CHUNKS, chips)),
            dma((CHUNKS, chips)),
            dma((CHUNKS,)),
            dma((CHUNKS,)),
            dma((CHUNKS,)),
            dma((CHUNKS,)),
            dma((CHUNKS, chips)),
            dma((CHUNKS, chips)),
            dma((sections,)),
            dma((sections,)),
            dma((CHUNKS, sections)),
            dma((CHUNKS, sections)),
        ],
        compiler_params=pltpu.CompilerParams(
            collective_id=0, has_side_effects=True, vmem_limit_bytes=48 * 1024 * 1024),
    )(route_tokens, gate, route_count, out_grad, saved_u, w_up_t, w_down)

    per_piece = CHUNKS
    block = width // per_piece
    return pl.pallas_call(
        functools.partial(gradient_kernel, (sections, slots, per_piece)),
        grid=(fold * per_piece,),
        out_shape=(
            jax.ShapeDtypeStruct((1, micro, tokens, features), jnp.bfloat16),
            jax.ShapeDtypeStruct((1, hid, features), jnp.bfloat16),
            jax.ShapeDtypeStruct((1, hid, features), jnp.bfloat16),
        ),
        in_specs=[
            pl.BlockSpec((hid, all_rows), lambda i: (0, 0)),
            pl.BlockSpec((hid, all_rows), lambda i: (0, 0)),
            pl.BlockSpec((all_rows, block), lambda i: (0, i)),
            pl.BlockSpec((1, micro, peers * cap, block), lambda i: (0, 0, 0, i)),
            pl.BlockSpec((micro, tokens, block), lambda i: (0, 0, i)),
            pl.BlockSpec((sections, TILE_ROWS, block), lambda i: (0, 0, i % per_piece)),
            pl.BlockSpec((micro * tokens, sections * TILE_ROWS), lambda i: (0, 0)),
        ],
        out_specs=(
            pl.BlockSpec((1, micro, tokens, block), lambda i: (0, 0, 0, i)),
            pl.BlockSpec((1, hid, block), lambda i: (0, 0, i)),
            pl.BlockSpec((1, hid, block), lambda i: (0, 0, i)),
        ),
        compiler_params=pltpu.CompilerParams(vmem_limit_bytes=32 * 1024 * 1024),
    )(hidden_t, activation_t, scaled, x_rows, out_grad, all_new, picks)


def solution(mesh):
    return jax.shard_map(
        functools.partial(per_device, mesh.shape["section"], mesh.shape["dp"]),
        mesh=mesh,
        in_specs=(
            P(None, "dp", None),
            P("section", None, None, None),
            P("section", None, None, "dp"),
            P("section", "dp", None),
            P("section", "dp", None),
            P("section", None, "dp"),
            P("section", None, "dp"),
            P("section", None, "dp"),
        ),
        out_specs=(
            P("section", None, "dp", None),
            P("section", "dp", None),
            P("section", "dp", None),
        ),
        check_vma=False,
    )
```

```python
import functools

import jax
import jax.numpy as jnp
from jax import lax
from jax.experimental import pallas as pl
from jax.experimental.pallas import tpu as pltpu
from jax.sharding import PartitionSpec as P

MESH = pl.DeviceIdType.MESH
TILE_ROWS = 16
CHUNKS = 2


def row_of_slot(index, peers, cap, micro):
    slot = index % (micro * cap)
    block = index // TILE_ROWS
    peer = block % (peers // 2) * 2 + block // (peers // 2)
    return (slot // cap) * (peers * cap) + peer * cap + slot % cap


def chain_kernel(
    sizes,
    token_hbm, gate_hbm, count_hbm, grad_hbm, saved_hbm, w_up_hbm, w_down_hbm,
    all_new_ref, picks_ref, scaled_ref, hidden_t_ref, activation_t_ref,
    token_ref, gate_ref, count_ref, grad_ref, saved_ref,
    w_up, w_down, gbuf, send_buf, pair_buf, sum_buf, recv_buf, new_buf, id_buf, cur_buf, slope_buf,
    load_sem, gather_send, gather_recv, share_send, share_recv, pair_send, pair_recv,
    reduce_send, reduce_recv, id_send, id_recv, new_send, new_recv,
):
    sections, peers, micro, cap = sizes
    slots = micro * cap
    fold = TILE_ROWS // slots
    section = lax.axis_index("section")
    me = lax.axis_index("dp")
    width = gbuf.shape[1]
    c_width = width // CHUNKS
    hid = w_down.shape[0]
    tokens = grad_ref.shape[1]
    span = micro * tokens
    rows = peers * TILE_ROWS
    chips = peers // 2
    half = chips * TILE_ROWS
    core = lax.rem(me, 2)
    chip = me // 2
    sibling = me + 1 - 2 * core

    small = [
        pltpu.make_async_copy(source, target, load_sem.at[2 + k])
        for k, (source, target) in enumerate((
            (token_hbm, token_ref), (gate_hbm, gate_ref), (count_hbm, count_ref),
            (grad_hbm, grad_ref), (saved_hbm, saved_ref)))
    ]
    for copy in small:
        copy.start()
    down_copy = pltpu.make_async_copy(w_down_hbm.at[0], w_down, load_sem.at[0])
    up_copy = pltpu.make_async_copy(w_up_hbm.at[0], w_up, load_sem.at[1])
    down_copy.start()

    def chip_at(k):
        return lax.rem(chip + k, chips)

    barrier = pltpu.get_barrier_semaphore()

    def greet(k, carry):
        pl.semaphore_signal(barrier, inc=1, device_id=(section, chip_at(k) * 2 + core), device_id_type=MESH)
        return carry

    lax.fori_loop(1, chips, greet, 0)
    pl.semaphore_signal(barrier, inc=1, device_id=(section, sibling), device_id_type=MESH)
    for k in range(1, sections):
        other = lax.rem(section + k, sections)
        pl.semaphore_signal(barrier, inc=1, device_id=(other, me), device_id_type=MESH)

    for copy in small:
        copy.wait()

    flat, weight = [], []
    for m in range(micro):
        for c in range(cap):
            flat.append(token_ref[0, m, c] + m * tokens)
            weight.append(jnp.where(c < count_ref[0, m, 0], gate_ref[0, m, c], jnp.float32(0.0)))
    sent = []
    for k in range(slots):
        mine = flat[k]
        for e in range(k):
            mine = jnp.where(flat[e] == flat[k], -sections * TILE_ROWS * span, mine)
        sent.append(mine)

    def spread(values, slot, start):
        out = start
        for k in range(slots):
            out = jnp.where(slot == k, values[k], out)
        return out

    row = lax.broadcasted_iota(jnp.int32, (TILE_ROWS, 128), 0)
    lane = lax.broadcasted_iota(jnp.int32, (8, 128), 1)
    lane_all = lax.broadcasted_iota(jnp.int32, (8, half), 1) % TILE_ROWS
    id_col = spread(flat, row % slots, jnp.zeros((TILE_ROWS, 128), jnp.int32)) + row // slots * span
    weight_col = spread(weight, row % slots, jnp.zeros((TILE_ROWS, 128), jnp.float32))
    id_row = spread(flat, lane_all % slots, jnp.zeros((8, half), jnp.int32)) + lane_all // slots * span
    sent_row = spread(sent, lane % slots, jnp.zeros((8, 128), jnp.int32)) + lane // slots * span
    id_buf[section] = jnp.where((lane < TILE_ROWS) & (sent_row >= 0), sent_row, -1)

    flat_col = id_col[:, :1] % span
    piece_col = lax.broadcasted_iota(jnp.int32, (TILE_ROWS, span), 0) // slots
    token_lane = lax.broadcasted_iota(jnp.int32, (TILE_ROWS, span), 1)
    base = jnp.zeros((TILE_ROWS, width), jnp.float32)
    for piece in range(fold):
        pick = jnp.where((token_lane == flat_col) & (piece_col == piece), 1.0, 0.0).astype(jnp.bfloat16)
        part = grad_ref[:, :, piece * width:(piece + 1) * width].reshape(span, width)
        base = base + jnp.dot(pick, part, preferred_element_type=jnp.float32)
    cur_buf[...] = base

    pl.semaphore_wait(barrier, chips + sections - 1)

    def id_copy(source, target):
        return pltpu.make_async_remote_copy(
            src_ref=id_buf.at[source], dst_ref=id_buf.at[source],
            send_sem=id_send.at[target], recv_sem=id_recv.at[source],
            device_id=(target, me), device_id_type=MESH)

    def columns_of(chunk):
        return pl.ds(chunk * c_width, c_width)

    def rows_of(peer):
        return pl.ds(pl.multiple_of(peer * TILE_ROWS, TILE_ROWS), TILE_ROWS)

    def new_copy(chunk, source, target):
        place = new_buf.at[source, :, columns_of(chunk)]
        return pltpu.make_async_remote_copy(
            src_ref=place, dst_ref=place,
            send_sem=new_send.at[chunk, target], recv_sem=new_recv.at[chunk, source],
            device_id=(target, me), device_id_type=MESH)

    def block_of(a_chip, a_core):
        return pl.ds(pl.multiple_of(a_core * half + a_chip * TILE_ROWS, TILE_ROWS), TILE_ROWS)

    def half_of(a_core):
        return pl.ds(pl.multiple_of(a_core * half, TILE_ROWS), half)

    def gather_copy(chunk, source, target):
        place = gbuf.at[block_of(source, core), columns_of(chunk)]
        return pltpu.make_async_remote_copy(
            src_ref=place, dst_ref=place,
            send_sem=gather_send.at[chunk, target], recv_sem=gather_recv.at[chunk, source],
            device_id=(section, target * 2 + core), device_id_type=MESH)

    def share_copy(chunk, a_core):
        place = gbuf.at[half_of(a_core), columns_of(chunk)]
        return pltpu.make_async_remote_copy(
            src_ref=place, dst_ref=place,
            send_sem=share_send.at[chunk], recv_sem=share_recv.at[chunk],
            device_id=(section, sibling), device_id_type=MESH)

    def pair_copy(chunk):
        return pltpu.make_async_remote_copy(
            src_ref=send_buf.at[half_of(1 - core), columns_of(chunk)],
            dst_ref=pair_buf.at[:, columns_of(chunk)],
            send_sem=pair_send.at[chunk], recv_sem=pair_recv.at[chunk],
            device_id=(section, sibling), device_id_type=MESH)

    def reduce_copy(chunk, source, target):
        return pltpu.make_async_remote_copy(
            src_ref=sum_buf.at[rows_of(target), columns_of(chunk)],
            dst_ref=recv_buf.at[rows_of(source), columns_of(chunk)],
            send_sem=reduce_send.at[chunk, target], recv_sem=reduce_recv.at[chunk, source],
            device_id=(section, target * 2 + core), device_id_type=MESH)

    for target in range(sections - 1):
        @pl.when(target < section)
        def _():
            id_copy(section, target).start()

    def take_newer(upper, columns):
        picks = jnp.where(id_col[:, :TILE_ROWS] == id_buf[upper][:1, :TILE_ROWS], 1.0, 0.0)
        hit = jnp.max(picks, axis=1, keepdims=True) > 0.5
        taken = jnp.dot(picks.astype(jnp.bfloat16), new_buf[upper, :, columns], preferred_element_type=jnp.float32)
        cur_buf[:, columns] = jnp.where(hit, taken, cur_buf[:, columns])

    for upper in range(sections - 1, 1, -1):
        @pl.when(upper > section + 1)
        def _():
            id_copy(upper, upper).wait_recv()
            for chunk in range(CHUNKS):
                new_copy(chunk, upper, upper).wait_recv()
            take_newer(upper, slice(0, width))

    above = lax.rem(section + 1, sections)
    has_above = section < sections - 1

    def prepare():
        for layer in range(sections):
            @pl.when(layer < section)
            def _():
                all_new_ref[layer] = jnp.zeros((TILE_ROWS, width), jnp.bfloat16)
                id_buf[layer] = jnp.full((8, 128), -1, jnp.int32)
        pre = saved_ref[0].reshape(slots * peers, hid).astype(jnp.float32)
        activation_t_ref[...] = (pre * jax.nn.sigmoid(pre)).T.astype(jnp.bfloat16)
        token = lax.broadcasted_iota(jnp.int32, (span, TILE_ROWS), 0)
        found = jnp.zeros((span, 1), jnp.float32)
        for layer in range(sections):
            ids = id_buf[layer][:1, :TILE_ROWS]
            same = jnp.where((token == ids % span) & (ids >= 0), 1.0, 0.0) * (1.0 - found)
            picks_ref[:, layer * TILE_ROWS:(layer + 1) * TILE_ROWS] = same
            found = jnp.maximum(found, jnp.max(same, axis=1, keepdims=True))

    @pl.when(has_above)
    def _():
        id_copy(above, above).wait_recv()
        prepare()

    my_rows = block_of(chip, core)
    for chunk in range(CHUNKS):
        columns = slice(chunk * c_width, (chunk + 1) * c_width)

        @pl.when(has_above)
        def _():
            new_copy(chunk, above, above).wait_recv()
            take_newer(above, columns)

        gbuf[my_rows, columns] = (weight_col[:, :1] * cur_buf[:, columns]).astype(jnp.bfloat16)

        def send(k, carry):
            gather_copy(chunk, chip, chip_at(k)).start()
            return carry

        lax.fori_loop(1, chips, send, 0)

    source = row_of_slot(lax.broadcasted_iota(jnp.int32, (rows, slots * peers), 0), peers, cap, micro)
    order = jnp.where(source == lax.broadcasted_iota(jnp.int32, (rows, slots * peers), 1), 1.0, 0.0)
    pre = jnp.dot(order.astype(jnp.bfloat16), saved_ref[0].reshape(slots * peers, hid), preferred_element_type=jnp.float32)
    sigmoid = jax.nn.sigmoid(pre)
    slope_buf[...] = sigmoid * (1.0 + pre * (1.0 - sigmoid))

    down_copy.wait()
    up_copy.start()
    row_piece = lax.broadcasted_iota(jnp.int32, (rows, c_width), 0) % TILE_ROWS // slots
    keep = [jnp.where(row_piece == piece, 1.0, 0.0).astype(jnp.bfloat16) for piece in range(fold)]
    total = jnp.zeros((hid, rows), jnp.float32)
    def pass_on(chunk):
        def arrive(k, carry):
            other = chip_at(k)
            gather_copy(chunk, other, other).wait_recv()
            return carry

        lax.fori_loop(1, chips, arrive, 0)
        share_copy(chunk, core).start()

    pass_on(0)
    for chunk in range(CHUNKS):
        if chunk + 1 < CHUNKS:
            pass_on(chunk + 1)
        share_copy(chunk, 1 - core).wait_recv()
        block = gbuf[:, chunk * c_width:(chunk + 1) * c_width]
        starts = [piece * width + chunk * c_width for piece in range(fold)]
        left = jnp.concatenate([w_down[:, start:start + c_width] for start in starts], axis=1)
        right = jnp.concatenate([block * keep[piece] for piece in range(fold)], axis=1)
        total = total + lax.dot_general(
            left, right, (((1,), (1,)), ((), ())), preferred_element_type=jnp.float32)

    back = total.T.reshape(peers, TILE_ROWS, hid)
    summed = back
    for k in range(1, fold):
        cut = k * slots
        summed = summed + jnp.concatenate([back[:, cut:], back[:, :cut]], axis=1)
    hidden = (summed.reshape(rows, hid) * slope_buf[...]).astype(jnp.bfloat16)

    def send_sums(chunk):
        columns = slice(chunk * c_width, (chunk + 1) * c_width)
        pair_copy(chunk).wait_recv()
        both = send_buf[half_of(core), columns].astype(jnp.float32) + pair_buf[:, columns].astype(jnp.float32)
        sum_buf[:, columns] = both.astype(jnp.bfloat16)

        def send(k, carry):
            reduce_copy(chunk, chip, chip_at(k)).start()
            return carry

        lax.fori_loop(1, chips, send, 0)
        recv_buf[rows_of(chip), columns] = sum_buf[rows_of(chip), columns]

    up_copy.wait()
    for chunk in range(CHUNKS):
        partial = jnp.zeros((rows, c_width), jnp.float32)
        for piece in range(fold):
            start = piece * width + chunk * c_width
            product = jnp.dot(hidden, w_up[:, start:start + c_width], preferred_element_type=jnp.float32)
            partial = jnp.where(row_piece == piece, product, partial)
        columns = slice(chunk * c_width, (chunk + 1) * c_width)
        send_buf[:, columns] = partial.astype(jnp.bfloat16)

        pair_copy(chunk).start()
        if chunk > 0:
            send_sums(chunk - 1)
    send_sums(CHUNKS - 1)

    source = row_of_slot(lax.broadcasted_iota(jnp.int32, (slots * peers, rows), 1), peers, cap, micro)
    order = jnp.where(source == lax.broadcasted_iota(jnp.int32, (slots * peers, rows), 0), 1.0, 0.0)
    piece_lane = lax.broadcasted_iota(jnp.int32, (slots * peers, rows), 1) % TILE_ROWS // slots
    for piece in range(fold):
        mine = jnp.where(piece_lane == piece, order, 0.0).astype(jnp.bfloat16)
        if piece == 0:
            hidden_t_ref[...] = jnp.dot(mine, hidden, preferred_element_type=jnp.float32).T.astype(jnp.bfloat16)
        scaled_ref[:, piece * width:(piece + 1) * width] = jnp.dot(
            mine, gbuf[...], preferred_element_type=jnp.float32).astype(jnp.bfloat16)
    for layer in range(sections):
        @pl.when(layer > section)
        def _():
            all_new_ref[layer] = new_buf[layer]

    alike = jnp.where(id_col[:, :1] == id_row[:1, :], 1.0, 0.0).astype(jnp.bfloat16)
    for chunk in range(CHUNKS):
        def arrive(k, carry):
            other = chip_at(k)
            reduce_copy(chunk, other, other).wait_recv()
            return carry

        lax.fori_loop(1, chips, arrive, 0)
        columns = slice(chunk * c_width, (chunk + 1) * c_width)
        delta = jnp.dot(alike, recv_buf[:, columns], preferred_element_type=jnp.float32)
        new_buf[section, :, columns] = (cur_buf[:, columns] + delta).astype(jnp.bfloat16)

        @pl.when(section > 0)
        def _():
            new_copy(chunk, section, section - 1).start()

    for target in range(sections - 2):
        @pl.when(target < section - 1)
        def _():
            for chunk in range(CHUNKS):
                new_copy(chunk, section, target).start()
    all_new_ref[section] = new_buf[section]

    @pl.when(jnp.logical_not(has_above))
    def _():
        prepare()

    def drain(k, carry):
        other = chip_at(k)
        for chunk in range(CHUNKS):
            gather_copy(chunk, chip, other).wait_send()
            reduce_copy(chunk, chip, other).wait_send()
        return carry

    lax.fori_loop(1, chips, drain, 0)
    for chunk in range(CHUNKS):
        share_copy(chunk, core).wait_send()
        pair_copy(chunk).wait_send()
    for target in range(sections - 1):
        @pl.when(target < section)
        def _():
            id_copy(section, target).wait_send()
            for chunk in range(CHUNKS):
                new_copy(chunk, section, target).wait_send()


def gradient_kernel(
    sizes,
    hidden_t_ref, activation_t_ref, scaled_ref, x_ref, grad_ref, new_ref, picks_ref,
    in_grad_ref, grad_up_ref, grad_down_ref,
):
    sections, slots, per_piece = sizes
    piece = pl.program_id(0) // per_piece
    span = grad_ref.shape[0] * grad_ref.shape[1]
    width = x_ref.shape[3]
    grad_down_ref[0] = jnp.dot(
        activation_t_ref[...], scaled_ref[...], preferred_element_type=jnp.float32).astype(jnp.bfloat16)
    grad_up_ref[0] = jnp.dot(
        hidden_t_ref[...], x_ref[0].reshape(-1, width), preferred_element_type=jnp.float32).astype(jnp.bfloat16)

    lane = lax.broadcasted_iota(jnp.int32, picks_ref.shape, 1)
    chosen = jnp.where(lane % TILE_ROWS // slots == piece, picks_ref[...], 0.0)
    hit = jnp.max(chosen, axis=1, keepdims=True) > 0.5
    newest = jnp.dot(
        chosen.astype(jnp.bfloat16), new_ref[...].reshape(sections * TILE_ROWS, width),
        preferred_element_type=jnp.float32)
    old = grad_ref[...].reshape(span, width).astype(jnp.float32)
    in_grad_ref[0] = jnp.where(hit, newest, old).astype(jnp.bfloat16).reshape(grad_ref.shape)


def per_device(sections, peers, out_grad, x_rows, saved_u, w_up_t, w_down, gate, route_tokens, route_count):
    micro, tokens, features = out_grad.shape
    cap = gate.shape[2]
    slots = micro * cap
    fold = TILE_ROWS // slots
    width = features // fold
    hid = w_down.shape[1]
    rows = peers * TILE_ROWS
    sizes = (sections, peers, micro, cap)

    vmem = pl.BlockSpec(memory_space=pltpu.VMEM)
    hbm = pl.BlockSpec(memory_space=pl.ANY)
    dma = pltpu.SemaphoreType.DMA
    half = rows // 2
    chips = peers // 2
    all_rows = peers * slots
    all_new, picks, scaled, hidden_t, activation_t = pl.pallas_call(
        functools.partial(chain_kernel, sizes),
        out_shape=(
            jax.ShapeDtypeStruct((sections, TILE_ROWS, width), jnp.bfloat16),
            jax.ShapeDtypeStruct((micro * tokens, sections * TILE_ROWS), jnp.float32),
            jax.ShapeDtypeStruct((all_rows, features), jnp.bfloat16),
            jax.ShapeDtypeStruct((hid, all_rows), jnp.bfloat16),
            jax.ShapeDtypeStruct((hid, all_rows), jnp.bfloat16),
        ),
        in_specs=[hbm] * 7,
        out_specs=(vmem,) * 5,
        scratch_shapes=[
            pltpu.SMEM(route_tokens.shape, jnp.int32),
            pltpu.SMEM(gate.shape, jnp.float32),
            pltpu.SMEM(route_count.shape, jnp.int32),
            pltpu.VMEM(out_grad.shape, jnp.bfloat16),
            pltpu.VMEM(saved_u.shape, jnp.bfloat16),
            pltpu.VMEM((hid, features), jnp.bfloat16),
            pltpu.VMEM((hid, features), jnp.bfloat16),
            pltpu.VMEM((rows, width), jnp.bfloat16),
            pltpu.VMEM((rows, width), jnp.bfloat16),
            pltpu.VMEM((half, width), jnp.bfloat16),
            pltpu.VMEM((half, width), jnp.bfloat16),
            pltpu.VMEM((half, width), jnp.bfloat16),
            pltpu.VMEM((sections, TILE_ROWS, width), jnp.bfloat16),
            pltpu.VMEM((sections, 8, 128), jnp.int32),
            pltpu.VMEM((TILE_ROWS, width), jnp.float32),
            pltpu.VMEM((rows, hid), jnp.float32),
            dma((7,)),
            dma((CHUNKS, chips)),
            dma((CHUNKS, chips)),
            dma((CHUNKS,)),
            dma((CHUNKS,)),
            dma((CHUNKS,)),
            dma((CHUNKS,)),
            dma((CHUNKS, chips)),
            dma((CHUNKS, chips)),
            dma((sections,)),
            dma((sections,)),
            dma((CHUNKS, sections)),
            dma((CHUNKS, sections)),
        ],
        compiler_params=pltpu.CompilerParams(
            collective_id=0, has_side_effects=True, vmem_limit_bytes=60 * 1024 * 1024),
    )(route_tokens, gate, route_count, out_grad, saved_u, w_up_t, w_down)

    per_piece = 3
    block = width // per_piece
    return pl.pallas_call(
        functools.partial(gradient_kernel, (sections, slots, per_piece)),
        grid=(fold * per_piece,),
        out_shape=(
            jax.ShapeDtypeStruct((1, micro, tokens, features), jnp.bfloat16),
            jax.ShapeDtypeStruct((1, hid, features), jnp.bfloat16),
            jax.ShapeDtypeStruct((1, hid, features), jnp.bfloat16),
        ),
        in_specs=[
            pl.BlockSpec((hid, all_rows), lambda i: (0, 0)),
            pl.BlockSpec((hid, all_rows), lambda i: (0, 0)),
            pl.BlockSpec((all_rows, block), lambda i: (0, i)),
            pl.BlockSpec((1, micro, peers * cap, block), lambda i: (0, 0, 0, i)),
            pl.BlockSpec((micro, tokens, block), lambda i: (0, 0, i)),
            pl.BlockSpec((sections, TILE_ROWS, block), lambda i: (0, 0, i % per_piece)),
            pl.BlockSpec((micro * tokens, sections * TILE_ROWS), lambda i: (0, 0)),
        ],
        out_specs=(
            pl.BlockSpec((1, micro, tokens, block), lambda i: (0, 0, 0, i)),
            pl.BlockSpec((1, hid, block), lambda i: (0, 0, i)),
            pl.BlockSpec((1, hid, block), lambda i: (0, 0, i)),
        ),
        compiler_params=pltpu.CompilerParams(vmem_limit_bytes=32 * 1024 * 1024),
    )(hidden_t, activation_t, scaled, x_rows, out_grad, all_new, picks)


def solution(mesh):
    return jax.shard_map(
        functools.partial(per_device, mesh.shape["section"], mesh.shape["dp"]),
        mesh=mesh,
        in_specs=(
            P(None, "dp", None),
            P("section", None, None, None),
            P("section", None, None, "dp"),
            P("section", "dp", None),
            P("section", "dp", None),
            P("section", None, "dp"),
            P("section", None, "dp"),
            P("section", None, "dp"),
        ),
        out_specs=(
            P("section", None, "dp", None),
            P("section", "dp", None),
            P("section", "dp", None),
        ),
        check_vma=False,
    )
```

```python
import functools

import jax
import jax.numpy as jnp
from jax import lax
from jax.experimental import pallas as pl
from jax.experimental.pallas import tpu as pltpu
from jax.sharding import PartitionSpec as P

MESH = pl.DeviceIdType.MESH
TILE_ROWS = 16
CHUNKS = 6


def row_of_slot(index, peers, cap, micro):
    slot = index % (micro * cap)
    block = index // TILE_ROWS
    peer = block % (peers // 2) * 2 + block // (peers // 2)
    return (slot // cap) * (peers * cap) + peer * cap + slot % cap


def chain_kernel(
    sizes,
    token_hbm, gate_hbm, count_hbm, grad_hbm, saved_hbm, w_up_hbm, w_down_hbm,
    all_new_ref, picks_ref, scaled_ref, hidden_t_ref, activation_t_ref,
    token_ref, gate_ref, count_ref, grad_ref, saved_ref,
    w_up, w_down, gbuf, send_buf, pair_buf, sum_buf, recv_buf, new_buf, id_buf, cur_buf, slope_buf,
    load_sem, gather_send, gather_recv, share_send, share_recv, pair_send, pair_recv,
    reduce_send, reduce_recv, id_send, id_recv, new_send, new_recv,
):
    sections, peers, micro, cap = sizes
    slots = micro * cap
    fold = TILE_ROWS // slots
    section = lax.axis_index("section")
    me = lax.axis_index("dp")
    width = gbuf.shape[1]
    c_width = width // CHUNKS
    hid = w_down.shape[0]
    tokens = grad_ref.shape[1]
    span = micro * tokens
    rows = peers * TILE_ROWS
    chips = peers // 2
    half = chips * TILE_ROWS
    core = lax.rem(me, 2)
    chip = me // 2
    sibling = me + 1 - 2 * core

    small = [
        pltpu.make_async_copy(source, target, load_sem.at[2 + k])
        for k, (source, target) in enumerate((
            (token_hbm, token_ref), (gate_hbm, gate_ref), (count_hbm, count_ref),
            (grad_hbm, grad_ref), (saved_hbm, saved_ref)))
    ]
    for copy in small:
        copy.start()
    down_copy = pltpu.make_async_copy(w_down_hbm.at[0], w_down, load_sem.at[0])
    up_copy = pltpu.make_async_copy(w_up_hbm.at[0], w_up, load_sem.at[1])
    down_copy.start()

    def chip_at(k):
        return lax.rem(chip + k, chips)

    barrier = pltpu.get_barrier_semaphore()

    def greet(k, carry):
        pl.semaphore_signal(barrier, inc=1, device_id=(section, chip_at(k) * 2 + core), device_id_type=MESH)
        return carry

    lax.fori_loop(1, chips, greet, 0)
    pl.semaphore_signal(barrier, inc=1, device_id=(section, sibling), device_id_type=MESH)
    for k in range(1, sections):
        other = lax.rem(section + k, sections)
        pl.semaphore_signal(barrier, inc=1, device_id=(other, me), device_id_type=MESH)

    for copy in small:
        copy.wait()

    flat, weight = [], []
    for m in range(micro):
        for c in range(cap):
            flat.append(token_ref[0, m, c] + m * tokens)
            weight.append(jnp.where(c < count_ref[0, 0, m], gate_ref[0, m, c], jnp.float32(0.0)))
    sent = []
    for k in range(slots):
        mine = flat[k]
        for e in range(k):
            mine = jnp.where(flat[e] == flat[k], -sections * TILE_ROWS * span, mine)
        sent.append(mine)

    def spread(values, slot, start):
        out = start
        for k in range(slots):
            out = jnp.where(slot == k, values[k], out)
        return out

    row = lax.broadcasted_iota(jnp.int32, (TILE_ROWS, 128), 0)
    lane = lax.broadcasted_iota(jnp.int32, (8, 128), 1)
    lane_all = lax.broadcasted_iota(jnp.int32, (8, half), 1) % TILE_ROWS
    id_col = spread(flat, row % slots, jnp.zeros((TILE_ROWS, 128), jnp.int32)) + row // slots * span
    weight_col = spread(weight, row % slots, jnp.zeros((TILE_ROWS, 128), jnp.float32))
    id_row = spread(flat, lane_all % slots, jnp.zeros((8, half), jnp.int32)) + lane_all // slots * span
    sent_row = spread(sent, lane % slots, jnp.zeros((8, 128), jnp.int32)) + lane // slots * span
    id_buf[section] = jnp.where((lane < TILE_ROWS) & (sent_row >= 0), sent_row, -1)

    flat_col = id_col[:, :1] % span
    piece_col = lax.broadcasted_iota(jnp.int32, (TILE_ROWS, span), 0) // slots
    token_lane = lax.broadcasted_iota(jnp.int32, (TILE_ROWS, span), 1)
    base = jnp.zeros((TILE_ROWS, width), jnp.float32)
    for piece in range(fold):
        pick = jnp.where((token_lane == flat_col) & (piece_col == piece), 1.0, 0.0).astype(jnp.bfloat16)
        part = grad_ref[:, :, piece * width:(piece + 1) * width].reshape(span, width)
        base = base + jnp.dot(pick, part, preferred_element_type=jnp.float32)
    cur_buf[...] = base

    pl.semaphore_wait(barrier, chips + sections - 1)

    def id_copy(source, target):
        return pltpu.make_async_remote_copy(
            src_ref=id_buf.at[source], dst_ref=id_buf.at[source],
            send_sem=id_send.at[target], recv_sem=id_recv.at[source],
            device_id=(target, me), device_id_type=MESH)

    def columns_of(chunk):
        return pl.ds(chunk * c_width, c_width)

    def rows_of(peer):
        return pl.ds(pl.multiple_of(peer * TILE_ROWS, TILE_ROWS), TILE_ROWS)

    def new_copy(chunk, source, target):
        place = new_buf.at[source, :, columns_of(chunk)]
        return pltpu.make_async_remote_copy(
            src_ref=place, dst_ref=place,
            send_sem=new_send.at[chunk, target], recv_sem=new_recv.at[chunk, source],
            device_id=(target, me), device_id_type=MESH)

    def block_of(a_chip, a_core):
        return pl.ds(pl.multiple_of(a_core * half + a_chip * TILE_ROWS, TILE_ROWS), TILE_ROWS)

    def half_of(a_core):
        return pl.ds(pl.multiple_of(a_core * half, TILE_ROWS), half)

    def gather_copy(chunk, source, target):
        place = gbuf.at[block_of(source, core), columns_of(chunk)]
        return pltpu.make_async_remote_copy(
            src_ref=place, dst_ref=place,
            send_sem=gather_send.at[chunk, target], recv_sem=gather_recv.at[chunk, source],
            device_id=(section, target * 2 + core), device_id_type=MESH)

    def share_copy(chunk, a_core):
        place = gbuf.at[half_of(a_core), columns_of(chunk)]
        return pltpu.make_async_remote_copy(
            src_ref=place, dst_ref=place,
            send_sem=share_send.at[chunk], recv_sem=share_recv.at[chunk],
            device_id=(section, sibling), device_id_type=MESH)

    def pair_copy(chunk):
        return pltpu.make_async_remote_copy(
            src_ref=send_buf.at[half_of(1 - core), columns_of(chunk)],
            dst_ref=pair_buf.at[:, columns_of(chunk)],
            send_sem=pair_send.at[chunk], recv_sem=pair_recv.at[chunk],
            device_id=(section, sibling), device_id_type=MESH)

    def reduce_copy(chunk, source, target):
        return pltpu.make_async_remote_copy(
            src_ref=sum_buf.at[rows_of(target), columns_of(chunk)],
            dst_ref=recv_buf.at[rows_of(source), columns_of(chunk)],
            send_sem=reduce_send.at[chunk, target], recv_sem=reduce_recv.at[chunk, source],
            device_id=(section, target * 2 + core), device_id_type=MESH)

    for target in range(sections - 1):
        @pl.when(target < section)
        def _():
            id_copy(section, target).start()

    def take_newer(upper, columns):
        picks = jnp.where(id_col[:, :TILE_ROWS] == id_buf[upper][:1, :TILE_ROWS], 1.0, 0.0)
        hit = jnp.max(picks, axis=1, keepdims=True) > 0.5
        taken = jnp.dot(picks.astype(jnp.bfloat16), new_buf[upper, :, columns], preferred_element_type=jnp.float32)
        cur_buf[:, columns] = jnp.where(hit, taken, cur_buf[:, columns])

    for upper in range(sections - 1, 1, -1):
        @pl.when(upper > section + 1)
        def _():
            id_copy(upper, upper).wait_recv()
            for chunk in range(CHUNKS):
                new_copy(chunk, upper, upper).wait_recv()
            take_newer(upper, slice(0, width))

    above = lax.rem(section + 1, sections)
    has_above = section < sections - 1

    def prepare():
        for layer in range(sections):
            @pl.when(layer < section)
            def _():
                all_new_ref[layer] = jnp.zeros((TILE_ROWS, width), jnp.bfloat16)
                id_buf[layer] = jnp.full((8, 128), -1, jnp.int32)
        pre = saved_ref[0].reshape(slots * peers, hid).astype(jnp.float32)
        activation_t_ref[...] = (pre * jax.nn.sigmoid(pre)).T.astype(jnp.bfloat16)
        token = lax.broadcasted_iota(jnp.int32, (span, TILE_ROWS), 0)
        found = jnp.zeros((span, 1), jnp.float32)
        for layer in range(sections):
            ids = id_buf[layer][:1, :TILE_ROWS]
            same = jnp.where((token == ids % span) & (ids >= 0), 1.0, 0.0) * (1.0 - found)
            picks_ref[:, layer * TILE_ROWS:(layer + 1) * TILE_ROWS] = same
            found = jnp.maximum(found, jnp.max(same, axis=1, keepdims=True))

    def find_slope():
        source = row_of_slot(lax.broadcasted_iota(jnp.int32, (rows, slots * peers), 0), peers, cap, micro)
        order = jnp.where(source == lax.broadcasted_iota(jnp.int32, (rows, slots * peers), 1), 1.0, 0.0)
        pre = jnp.dot(order.astype(jnp.bfloat16), saved_ref[0].reshape(slots * peers, hid), preferred_element_type=jnp.float32)
        sigmoid = jax.nn.sigmoid(pre)
        slope_buf[...] = sigmoid * (1.0 + pre * (1.0 - sigmoid))

    @pl.when(has_above)
    def _():
        find_slope()
        id_copy(above, above).wait_recv()
        prepare()

    my_rows = block_of(chip, core)
    for chunk in range(CHUNKS):
        columns = slice(chunk * c_width, (chunk + 1) * c_width)

        @pl.when(has_above)
        def _():
            new_copy(chunk, above, above).wait_recv()
            take_newer(above, columns)

        gbuf[my_rows, columns] = (weight_col[:, :1] * cur_buf[:, columns]).astype(jnp.bfloat16)

        def send(k, carry):
            gather_copy(chunk, chip, chip_at(k)).start()
            return carry

        lax.fori_loop(1, chips, send, 0)

    @pl.when(jnp.logical_not(has_above))
    def _():
        find_slope()

    down_copy.wait()
    up_copy.start()
    row_piece = lax.broadcasted_iota(jnp.int32, (rows, c_width), 0) % TILE_ROWS // slots
    keep = [jnp.where(row_piece == piece, 1.0, 0.0).astype(jnp.bfloat16) for piece in range(fold)]
    total = jnp.zeros((hid, rows), jnp.float32)
    def pass_on(chunk):
        def arrive(k, carry):
            other = chip_at(k)
            gather_copy(chunk, other, other).wait_recv()
            return carry

        lax.fori_loop(1, chips, arrive, 0)
        share_copy(chunk, core).start()

    pass_on(0)
    for chunk in range(CHUNKS):
        if chunk + 1 < CHUNKS:
            pass_on(chunk + 1)
        share_copy(chunk, 1 - core).wait_recv()
        block = gbuf[:, chunk * c_width:(chunk + 1) * c_width]
        starts = [piece * width + chunk * c_width for piece in range(fold)]
        left = jnp.concatenate([w_down[:, start:start + c_width] for start in starts], axis=1)
        right = jnp.concatenate([block * keep[piece] for piece in range(fold)], axis=1)
        total = total + lax.dot_general(
            left, right, (((1,), (1,)), ((), ())), preferred_element_type=jnp.float32)

    back = total.T.reshape(peers, TILE_ROWS, hid)
    summed = back
    for k in range(1, fold):
        cut = k * slots
        summed = summed + jnp.concatenate([back[:, cut:], back[:, :cut]], axis=1)
    hidden = (summed.reshape(rows, hid) * slope_buf[...]).astype(jnp.bfloat16)

    def send_sums(chunk):
        columns = slice(chunk * c_width, (chunk + 1) * c_width)
        pair_copy(chunk).wait_recv()
        both = send_buf[half_of(core), columns].astype(jnp.float32) + pair_buf[:, columns].astype(jnp.float32)
        sum_buf[:, columns] = both.astype(jnp.bfloat16)

        def send(k, carry):
            reduce_copy(chunk, chip, chip_at(k)).start()
            return carry

        lax.fori_loop(1, chips, send, 0)
        recv_buf[rows_of(chip), columns] = sum_buf[rows_of(chip), columns]

    up_copy.wait()
    for chunk in range(CHUNKS):
        partial = jnp.zeros((rows, c_width), jnp.float32)
        for piece in range(fold):
            start = piece * width + chunk * c_width
            product = jnp.dot(hidden, w_up[:, start:start + c_width], preferred_element_type=jnp.float32)
            partial = jnp.where(row_piece == piece, product, partial)
        columns = slice(chunk * c_width, (chunk + 1) * c_width)
        send_buf[:, columns] = partial.astype(jnp.bfloat16)

        pair_copy(chunk).start()
        if chunk > 0:
            send_sums(chunk - 1)
    send_sums(CHUNKS - 1)

    def keep_rows():
        source = row_of_slot(lax.broadcasted_iota(jnp.int32, (slots * peers, rows), 1), peers, cap, micro)
        order = jnp.where(source == lax.broadcasted_iota(jnp.int32, (slots * peers, rows), 0), 1.0, 0.0)
        piece_lane = lax.broadcasted_iota(jnp.int32, (slots * peers, rows), 1) % TILE_ROWS // slots
        for piece in range(fold):
            mine = jnp.where(piece_lane == piece, order, 0.0).astype(jnp.bfloat16)
            if piece == 0:
                hidden_t_ref[...] = jnp.dot(mine, hidden, preferred_element_type=jnp.float32).T.astype(jnp.bfloat16)
            scaled_ref[:, piece * width:(piece + 1) * width] = jnp.dot(
                mine, gbuf[...], preferred_element_type=jnp.float32).astype(jnp.bfloat16)
        for layer in range(sections):
            @pl.when(layer > section)
            def _():
                all_new_ref[layer] = new_buf[layer]

    @pl.when(section == 0)
    def _():
        keep_rows()

    alike = jnp.where(id_col[:, :1] == id_row[:1, :], 1.0, 0.0).astype(jnp.bfloat16)
    for chunk in range(CHUNKS):
        def arrive(k, carry):
            other = chip_at(k)
            reduce_copy(chunk, other, other).wait_recv()
            return carry

        lax.fori_loop(1, chips, arrive, 0)
        columns = slice(chunk * c_width, (chunk + 1) * c_width)
        delta = jnp.dot(alike, recv_buf[:, columns], preferred_element_type=jnp.float32)
        new_buf[section, :, columns] = (cur_buf[:, columns] + delta).astype(jnp.bfloat16)

        @pl.when(section > 0)
        def _():
            new_copy(chunk, section, section - 1).start()

    for target in range(sections - 2):
        @pl.when(target < section - 1)
        def _():
            for chunk in range(CHUNKS):
                new_copy(chunk, section, target).start()
    all_new_ref[section] = new_buf[section]

    @pl.when(section > 0)
    def _():
        keep_rows()


    @pl.when(jnp.logical_not(has_above))
    def _():
        prepare()

    def drain(k, carry):
        other = chip_at(k)
        for chunk in range(CHUNKS):
            gather_copy(chunk, chip, other).wait_send()
            reduce_copy(chunk, chip, other).wait_send()
        return carry

    lax.fori_loop(1, chips, drain, 0)
    for chunk in range(CHUNKS):
        share_copy(chunk, core).wait_send()
        pair_copy(chunk).wait_send()
    for target in range(sections - 1):
        @pl.when(target < section)
        def _():
            id_copy(section, target).wait_send()
            for chunk in range(CHUNKS):
                new_copy(chunk, section, target).wait_send()


def gradient_kernel(
    sizes,
    hidden_t_ref, activation_t_ref, scaled_ref, x_ref, grad_ref, new_ref, picks_ref,
    in_grad_ref, grad_up_ref, grad_down_ref,
):
    sections, slots, per_piece = sizes
    piece = pl.program_id(0) // per_piece
    span = grad_ref.shape[0] * grad_ref.shape[1]
    width = x_ref.shape[3]
    grad_down_ref[0] = jnp.dot(
        activation_t_ref[...], scaled_ref[...], preferred_element_type=jnp.float32).astype(jnp.bfloat16)
    grad_up_ref[0] = jnp.dot(
        hidden_t_ref[...], x_ref[0].reshape(-1, width), preferred_element_type=jnp.float32).astype(jnp.bfloat16)

    lane = lax.broadcasted_iota(jnp.int32, picks_ref.shape, 1)
    chosen = jnp.where(lane % TILE_ROWS // slots == piece, picks_ref[...], 0.0)
    hit = jnp.max(chosen, axis=1, keepdims=True) > 0.5
    newest = jnp.dot(
        chosen.astype(jnp.bfloat16), new_ref[...].reshape(sections * TILE_ROWS, width),
        preferred_element_type=jnp.float32)
    old = grad_ref[...].reshape(span, width).astype(jnp.float32)
    in_grad_ref[0] = jnp.where(hit, newest, old).astype(jnp.bfloat16).reshape(grad_ref.shape)


def per_device(sections, peers, out_grad, x_rows, saved_u, w_up_t, w_down, gate, route_tokens, route_count):
    micro, tokens, features = out_grad.shape
    cap = gate.shape[2]
    slots = micro * cap
    fold = TILE_ROWS // slots
    width = features // fold
    hid = w_down.shape[1]
    rows = peers * TILE_ROWS
    sizes = (sections, peers, micro, cap)

    vmem = pl.BlockSpec(memory_space=pltpu.VMEM)
    hbm = pl.BlockSpec(memory_space=pl.ANY)
    dma = pltpu.SemaphoreType.DMA
    half = rows // 2
    chips = peers // 2
    all_rows = peers * slots
    all_new, picks, scaled, hidden_t, activation_t = pl.pallas_call(
        functools.partial(chain_kernel, sizes),
        out_shape=(
            jax.ShapeDtypeStruct((sections, TILE_ROWS, width), jnp.bfloat16),
            jax.ShapeDtypeStruct((micro * tokens, sections * TILE_ROWS), jnp.float32),
            jax.ShapeDtypeStruct((all_rows, features), jnp.bfloat16),
            jax.ShapeDtypeStruct((hid, all_rows), jnp.bfloat16),
            jax.ShapeDtypeStruct((hid, all_rows), jnp.bfloat16),
        ),
        in_specs=[hbm] * 7,
        out_specs=(vmem,) * 5,
        scratch_shapes=[
            pltpu.SMEM(route_tokens.shape, jnp.int32),
            pltpu.SMEM(gate.shape, jnp.float32),
            pltpu.SMEM((1, 1, micro), jnp.int32),
            pltpu.VMEM(out_grad.shape, jnp.bfloat16),
            pltpu.VMEM(saved_u.shape, jnp.bfloat16),
            pltpu.VMEM((hid, features), jnp.bfloat16),
            pltpu.VMEM((hid, features), jnp.bfloat16),
            pltpu.VMEM((rows, width), jnp.bfloat16),
            pltpu.VMEM((rows, width), jnp.bfloat16),
            pltpu.VMEM((half, width), jnp.bfloat16),
            pltpu.VMEM((half, width), jnp.bfloat16),
            pltpu.VMEM((half, width), jnp.bfloat16),
            pltpu.VMEM((sections, TILE_ROWS, width), jnp.bfloat16),
            pltpu.VMEM((sections, 8, 128), jnp.int32),
            pltpu.VMEM((TILE_ROWS, width), jnp.float32),
            pltpu.VMEM((rows, hid), jnp.float32),
            dma((7,)),
            dma((CHUNKS, chips)),
            dma((CHUNKS, chips)),
            dma((CHUNKS,)),
            dma((CHUNKS,)),
            dma((CHUNKS,)),
            dma((CHUNKS,)),
            dma((CHUNKS, chips)),
            dma((CHUNKS, chips)),
            dma((sections,)),
            dma((sections,)),
            dma((CHUNKS, sections)),
            dma((CHUNKS, sections)),
        ],
        compiler_params=pltpu.CompilerParams(
            collective_id=0, has_side_effects=True, vmem_limit_bytes=60 * 1024 * 1024),
    )(route_tokens, gate, route_count.transpose(0, 2, 1), out_grad, saved_u, w_up_t, w_down)

    per_piece = 2
    block = width // per_piece
    return pl.pallas_call(
        functools.partial(gradient_kernel, (sections, slots, per_piece)),
        grid=(fold * per_piece,),
        out_shape=(
            jax.ShapeDtypeStruct((1, micro, tokens, features), jnp.bfloat16),
            jax.ShapeDtypeStruct((1, hid, features), jnp.bfloat16),
            jax.ShapeDtypeStruct((1, hid, features), jnp.bfloat16),
        ),
        in_specs=[
            pl.BlockSpec((hid, all_rows), lambda i: (0, 0)),
            pl.BlockSpec((hid, all_rows), lambda i: (0, 0)),
            pl.BlockSpec((all_rows, block), lambda i: (0, i)),
            pl.BlockSpec((1, micro, peers * cap, block), lambda i: (0, 0, 0, i)),
            pl.BlockSpec((micro, tokens, block), lambda i: (0, 0, i)),
            pl.BlockSpec((sections, TILE_ROWS, block), lambda i: (0, 0, i % per_piece)),
            pl.BlockSpec((micro * tokens, sections * TILE_ROWS), lambda i: (0, 0)),
        ],
        out_specs=(
            pl.BlockSpec((1, micro, tokens, block), lambda i: (0, 0, 0, i)),
            pl.BlockSpec((1, hid, block), lambda i: (0, 0, i)),
            pl.BlockSpec((1, hid, block), lambda i: (0, 0, i)),
        ),
        compiler_params=pltpu.CompilerParams(vmem_limit_bytes=60 * 1024 * 1024),
    )(hidden_t, activation_t, scaled, x_rows, out_grad, all_new, picks)


def solution(mesh):
    return jax.shard_map(
        functools.partial(per_device, mesh.shape["section"], mesh.shape["dp"]),
        mesh=mesh,
        in_specs=(
            P(None, "dp", None),
            P("section", None, None, None),
            P("section", None, None, "dp"),
            P("section", "dp", None),
            P("section", "dp", None),
            P("section", None, "dp"),
            P("section", None, "dp"),
            P("section", None, "dp"),
        ),
        out_specs=(
            P("section", None, "dp", None),
            P("section", "dp", None),
            P("section", "dp", None),
        ),
        check_vma=False,
    )
```

```python
import functools

import jax
import jax.numpy as jnp
from jax import lax
from jax.experimental import pallas as pl
from jax.experimental.pallas import tpu as pltpu
from jax.sharding import PartitionSpec as P

MESH = pl.DeviceIdType.MESH
TILE_ROWS = 16
CHUNKS = 3


def row_of_slot(index, peers, cap, micro):
    slot = index % (micro * cap)
    block = index // TILE_ROWS
    peer = block % (peers // 2) * 2 + block // (peers // 2)
    return (slot // cap) * (peers * cap) + peer * cap + slot % cap


def chain_kernel(
    sizes,
    token_hbm, gate_hbm, count_hbm, grad_hbm, saved_hbm, w_up_hbm, w_down_hbm,
    all_new_ref, picks_ref, scaled_ref, hidden_t_ref, activation_t_ref,
    token_ref, gate_ref, count_ref, grad_ref, saved_ref,
    w_up, w_down, gbuf, send_buf, pair_buf, sum_buf, recv_buf, new_buf, id_buf, cur_buf, slope_buf,
    load_sem, gather_send, gather_recv, share_send, share_recv, pair_send, pair_recv,
    reduce_send, reduce_recv, id_send, id_recv, new_send, new_recv,
):
    sections, peers, micro, cap = sizes
    slots = micro * cap
    fold = TILE_ROWS // slots
    section = lax.axis_index("section")
    me = lax.axis_index("dp")
    width = gbuf.shape[1]
    c_width = width // CHUNKS
    hid = w_down.shape[0]
    tokens = grad_ref.shape[1]
    span = micro * tokens
    rows = peers * TILE_ROWS
    chips = peers // 2
    half = chips * TILE_ROWS
    core = lax.rem(me, 2)
    chip = me // 2
    sibling = me + 1 - 2 * core

    small = [
        pltpu.make_async_copy(source, target, load_sem.at[2 + k])
        for k, (source, target) in enumerate((
            (token_hbm, token_ref), (gate_hbm, gate_ref), (count_hbm, count_ref),
            (grad_hbm, grad_ref), (saved_hbm, saved_ref)))
    ]
    for copy in small:
        copy.start()
    down_copy = pltpu.make_async_copy(w_down_hbm.at[0], w_down, load_sem.at[0])
    up_copy = pltpu.make_async_copy(w_up_hbm.at[0], w_up, load_sem.at[1])
    down_copy.start()

    def chip_at(k):
        return lax.rem(chip + k, chips)

    barrier = pltpu.get_barrier_semaphore()

    def greet(k, carry):
        pl.semaphore_signal(barrier, inc=1, device_id=(section, chip_at(k) * 2 + core), device_id_type=MESH)
        return carry

    lax.fori_loop(1, chips, greet, 0)
    pl.semaphore_signal(barrier, inc=1, device_id=(section, sibling), device_id_type=MESH)
    for k in range(1, sections):
        other = lax.rem(section + k, sections)
        pl.semaphore_signal(barrier, inc=1, device_id=(other, me), device_id_type=MESH)

    for copy in small:
        copy.wait()

    flat, weight = [], []
    for m in range(micro):
        for c in range(cap):
            flat.append(token_ref[0, m, c] + m * tokens)
            weight.append(jnp.where(c < count_ref[0, 0, m], gate_ref[0, m, c], jnp.float32(0.0)))
    sent = []
    for k in range(slots):
        mine = flat[k]
        for e in range(k):
            mine = jnp.where(flat[e] == flat[k], -sections * TILE_ROWS * span, mine)
        sent.append(mine)

    def spread(values, slot, start):
        out = start
        for k in range(slots):
            out = jnp.where(slot == k, values[k], out)
        return out

    row = lax.broadcasted_iota(jnp.int32, (TILE_ROWS, 128), 0)
    lane = lax.broadcasted_iota(jnp.int32, (8, 128), 1)
    lane_all = lax.broadcasted_iota(jnp.int32, (8, half), 1) % TILE_ROWS
    id_col = spread(flat, row % slots, jnp.zeros((TILE_ROWS, 128), jnp.int32)) + row // slots * span
    weight_col = spread(weight, row % slots, jnp.zeros((TILE_ROWS, 128), jnp.float32))
    id_row = spread(flat, lane_all % slots, jnp.zeros((8, half), jnp.int32)) + lane_all // slots * span
    sent_row = spread(sent, lane % slots, jnp.zeros((8, 128), jnp.int32)) + lane // slots * span
    id_buf[section] = jnp.where((lane < TILE_ROWS) & (sent_row >= 0), sent_row, -1)

    flat_col = id_col[:, :1] % span
    piece_col = lax.broadcasted_iota(jnp.int32, (TILE_ROWS, span), 0) // slots
    token_lane = lax.broadcasted_iota(jnp.int32, (TILE_ROWS, span), 1)
    base = jnp.zeros((TILE_ROWS, width), jnp.float32)
    for piece in range(fold):
        pick = jnp.where((token_lane == flat_col) & (piece_col == piece), 1.0, 0.0).astype(jnp.bfloat16)
        part = grad_ref[:, :, piece * width:(piece + 1) * width].reshape(span, width)
        base = base + jnp.dot(pick, part, preferred_element_type=jnp.float32)
    cur_buf[...] = base

    pl.semaphore_wait(barrier, chips + sections - 1)

    def id_copy(source, target):
        return pltpu.make_async_remote_copy(
            src_ref=id_buf.at[source], dst_ref=id_buf.at[source],
            send_sem=id_send.at[target], recv_sem=id_recv.at[source],
            device_id=(target, me), device_id_type=MESH)

    def columns_of(chunk):
        return pl.ds(chunk * c_width, c_width)

    def rows_of(peer):
        return pl.ds(pl.multiple_of(peer * TILE_ROWS, TILE_ROWS), TILE_ROWS)

    def new_copy(chunk, source, target):
        place = new_buf.at[source, :, columns_of(chunk)]
        return pltpu.make_async_remote_copy(
            src_ref=place, dst_ref=place,
            send_sem=new_send.at[chunk, target], recv_sem=new_recv.at[chunk, source],
            device_id=(target, me), device_id_type=MESH)

    def block_of(a_chip, a_core):
        return pl.ds(pl.multiple_of(a_core * half + a_chip * TILE_ROWS, TILE_ROWS), TILE_ROWS)

    def half_of(a_core):
        return pl.ds(pl.multiple_of(a_core * half, TILE_ROWS), half)

    def gather_copy(chunk, source, target):
        place = gbuf.at[block_of(source, core), columns_of(chunk)]
        return pltpu.make_async_remote_copy(
            src_ref=place, dst_ref=place,
            send_sem=gather_send.at[chunk, target], recv_sem=gather_recv.at[chunk, source],
            device_id=(section, target * 2 + core), device_id_type=MESH)

    def share_copy(chunk, a_core):
        place = gbuf.at[half_of(a_core), columns_of(chunk)]
        return pltpu.make_async_remote_copy(
            src_ref=place, dst_ref=place,
            send_sem=share_send.at[chunk], recv_sem=share_recv.at[chunk],
            device_id=(section, sibling), device_id_type=MESH)

    def pair_copy(chunk):
        return pltpu.make_async_remote_copy(
            src_ref=send_buf.at[half_of(1 - core), columns_of(chunk)],
            dst_ref=pair_buf.at[:, columns_of(chunk)],
            send_sem=pair_send.at[chunk], recv_sem=pair_recv.at[chunk],
            device_id=(section, sibling), device_id_type=MESH)

    def reduce_copy(chunk, source, target):
        return pltpu.make_async_remote_copy(
            src_ref=sum_buf.at[rows_of(target), columns_of(chunk)],
            dst_ref=recv_buf.at[rows_of(source), columns_of(chunk)],
            send_sem=reduce_send.at[chunk, target], recv_sem=reduce_recv.at[chunk, source],
            device_id=(section, target * 2 + core), device_id_type=MESH)

    for target in range(sections - 1):
        @pl.when(target < section)
        def _():
            id_copy(section, target).start()

    def take_newer(upper, columns):
        picks = jnp.where(id_col[:, :TILE_ROWS] == id_buf[upper][:1, :TILE_ROWS], 1.0, 0.0)
        hit = jnp.max(picks, axis=1, keepdims=True) > 0.5
        taken = jnp.dot(picks.astype(jnp.bfloat16), new_buf[upper, :, columns], preferred_element_type=jnp.float32)
        cur_buf[:, columns] = jnp.where(hit, taken, cur_buf[:, columns])

    for upper in range(sections - 1, 1, -1):
        @pl.when(upper > section + 1)
        def _():
            id_copy(upper, upper).wait_recv()
            for chunk in range(CHUNKS):
                new_copy(chunk, upper, upper).wait_recv()
            take_newer(upper, slice(0, width))

    above = lax.rem(section + 1, sections)
    has_above = section < sections - 1

    def prepare():
        for layer in range(sections):
            @pl.when(layer < section)
            def _():
                all_new_ref[layer] = jnp.zeros((TILE_ROWS, width), jnp.bfloat16)
                id_buf[layer] = jnp.full((8, 128), -1, jnp.int32)
        pre = saved_ref[0].reshape(slots * peers, hid).astype(jnp.float32)
        activation_t_ref[...] = (pre * jax.nn.sigmoid(pre)).T.astype(jnp.bfloat16)
        token = lax.broadcasted_iota(jnp.int32, (span, TILE_ROWS), 0)
        found = jnp.zeros((span, 1), jnp.float32)
        for layer in range(sections):
            ids = id_buf[layer][:1, :TILE_ROWS]
            same = jnp.where((token == ids % span) & (ids >= 0), 1.0, 0.0) * (1.0 - found)
            picks_ref[:, layer * TILE_ROWS:(layer + 1) * TILE_ROWS] = same
            found = jnp.maximum(found, jnp.max(same, axis=1, keepdims=True))

    def find_slope():
        source = row_of_slot(lax.broadcasted_iota(jnp.int32, (rows, slots * peers), 0), peers, cap, micro)
        order = jnp.where(source == lax.broadcasted_iota(jnp.int32, (rows, slots * peers), 1), 1.0, 0.0)
        pre = jnp.dot(order.astype(jnp.bfloat16), saved_ref[0].reshape(slots * peers, hid), preferred_element_type=jnp.float32)
        sigmoid = jax.nn.sigmoid(pre)
        slope_buf[...] = sigmoid * (1.0 + pre * (1.0 - sigmoid))

    @pl.when(has_above)
    def _():
        find_slope()
        id_copy(above, above).wait_recv()
        prepare()

    my_rows = block_of(chip, core)
    for chunk in range(CHUNKS):
        columns = slice(chunk * c_width, (chunk + 1) * c_width)

        @pl.when(has_above)
        def _():
            new_copy(chunk, above, above).wait_recv()
            take_newer(above, columns)

        gbuf[my_rows, columns] = (weight_col[:, :1] * cur_buf[:, columns]).astype(jnp.bfloat16)

        def send(k, carry):
            gather_copy(chunk, chip, chip_at(k)).start()
            return carry

        lax.fori_loop(1, chips, send, 0)

    @pl.when(jnp.logical_not(has_above))
    def _():
        find_slope()

    down_copy.wait()
    up_copy.start()
    row_piece = lax.broadcasted_iota(jnp.int32, (rows, c_width), 0) % TILE_ROWS // slots
    keep = [jnp.where(row_piece == piece, 1.0, 0.0).astype(jnp.bfloat16) for piece in range(fold)]
    total = jnp.zeros((hid, rows), jnp.float32)
    def pass_on(chunk):
        def arrive(k, carry):
            other = chip_at(k)
            gather_copy(chunk, other, other).wait_recv()
            return carry

        lax.fori_loop(1, chips, arrive, 0)
        share_copy(chunk, core).start()

    pass_on(0)
    for chunk in range(CHUNKS):
        if chunk + 1 < CHUNKS:
            pass_on(chunk + 1)
        share_copy(chunk, 1 - core).wait_recv()
        block = gbuf[:, chunk * c_width:(chunk + 1) * c_width]
        starts = [piece * width + chunk * c_width for piece in range(fold)]
        left = jnp.concatenate([w_down[:, start:start + c_width] for start in starts], axis=1)
        right = jnp.concatenate([block * keep[piece] for piece in range(fold)], axis=1)
        total = total + lax.dot_general(
            left, right, (((1,), (1,)), ((), ())), preferred_element_type=jnp.float32)

    back = total.T.reshape(peers, TILE_ROWS, hid)
    summed = back
    for k in range(1, fold):
        cut = k * slots
        summed = summed + jnp.concatenate([back[:, cut:], back[:, :cut]], axis=1)
    hidden = (summed.reshape(rows, hid) * slope_buf[...]).astype(jnp.bfloat16)

    def send_sums(chunk):
        columns = slice(chunk * c_width, (chunk + 1) * c_width)
        pair_copy(chunk).wait_recv()
        both = send_buf[half_of(core), columns].astype(jnp.float32) + pair_buf[:, columns].astype(jnp.float32)
        sum_buf[:, columns] = both.astype(jnp.bfloat16)

        def send(k, carry):
            reduce_copy(chunk, chip, chip_at(k)).start()
            return carry

        lax.fori_loop(1, chips, send, 0)
        recv_buf[rows_of(chip), columns] = sum_buf[rows_of(chip), columns]

    up_copy.wait()
    for chunk in range(CHUNKS):
        partial = jnp.zeros((rows, c_width), jnp.float32)
        for piece in range(fold):
            start = piece * width + chunk * c_width
            product = jnp.dot(hidden, w_up[:, start:start + c_width], preferred_element_type=jnp.float32)
            partial = jnp.where(row_piece == piece, product, partial)
        columns = slice(chunk * c_width, (chunk + 1) * c_width)
        send_buf[:, columns] = partial.astype(jnp.bfloat16)

        pair_copy(chunk).start()
        if chunk > 0:
            send_sums(chunk - 1)
    send_sums(CHUNKS - 1)

    def keep_rows():
        source = row_of_slot(lax.broadcasted_iota(jnp.int32, (slots * peers, rows), 1), peers, cap, micro)
        order = jnp.where(source == lax.broadcasted_iota(jnp.int32, (slots * peers, rows), 0), 1.0, 0.0)
        piece_lane = lax.broadcasted_iota(jnp.int32, (slots * peers, rows), 1) % TILE_ROWS // slots
        for piece in range(fold):
            mine = jnp.where(piece_lane == piece, order, 0.0).astype(jnp.bfloat16)
            if piece == 0:
                hidden_t_ref[...] = jnp.dot(mine, hidden, preferred_element_type=jnp.float32).T.astype(jnp.bfloat16)
            scaled_ref[:, piece * width:(piece + 1) * width] = jnp.dot(
                mine, gbuf[...], preferred_element_type=jnp.float32).astype(jnp.bfloat16)
        for layer in range(sections):
            @pl.when(layer > section)
            def _():
                all_new_ref[layer] = new_buf[layer]

    @pl.when(section == 0)
    def _():
        keep_rows()

    alike = jnp.where(id_col[:, :1] == id_row[:1, :], 1.0, 0.0).astype(jnp.bfloat16)
    for chunk in range(CHUNKS):
        def arrive(k, carry):
            other = chip_at(k)
            reduce_copy(chunk, other, other).wait_recv()
            return carry

        lax.fori_loop(1, chips, arrive, 0)
        columns = slice(chunk * c_width, (chunk + 1) * c_width)
        delta = jnp.dot(alike, recv_buf[:, columns], preferred_element_type=jnp.float32)
        new_buf[section, :, columns] = (cur_buf[:, columns] + delta).astype(jnp.bfloat16)

        @pl.when(section > 0)
        def _():
            new_copy(chunk, section, section - 1).start()

    for target in range(sections - 2):
        @pl.when(target < section - 1)
        def _():
            for chunk in range(CHUNKS):
                new_copy(chunk, section, target).start()
    all_new_ref[section] = new_buf[section]

    @pl.when(section > 0)
    def _():
        keep_rows()


    @pl.when(jnp.logical_not(has_above))
    def _():
        prepare()

    def drain(k, carry):
        other = chip_at(k)
        for chunk in range(CHUNKS):
            gather_copy(chunk, chip, other).wait_send()
            reduce_copy(chunk, chip, other).wait_send()
        return carry

    lax.fori_loop(1, chips, drain, 0)
    for chunk in range(CHUNKS):
        share_copy(chunk, core).wait_send()
        pair_copy(chunk).wait_send()
    for target in range(sections - 1):
        @pl.when(target < section)
        def _():
            id_copy(section, target).wait_send()
            for chunk in range(CHUNKS):
                new_copy(chunk, section, target).wait_send()


def gradient_kernel(
    sizes,
    hidden_t_ref, activation_t_ref, scaled_ref, x_ref, grad_ref, new_ref, picks_ref,
    in_grad_ref, grad_up_ref, grad_down_ref,
):
    sections, slots, per_piece = sizes
    piece = pl.program_id(0) // per_piece
    span = grad_ref.shape[0] * grad_ref.shape[1]
    width = x_ref.shape[3]
    grad_down_ref[0] = jnp.dot(
        activation_t_ref[...], scaled_ref[...], preferred_element_type=jnp.float32).astype(jnp.bfloat16)
    grad_up_ref[0] = jnp.dot(
        hidden_t_ref[...], x_ref[0].reshape(-1, width), preferred_element_type=jnp.float32).astype(jnp.bfloat16)

    lane = lax.broadcasted_iota(jnp.int32, picks_ref.shape, 1)
    chosen = jnp.where(lane % TILE_ROWS // slots == piece, picks_ref[...], 0.0)
    hit = jnp.max(chosen, axis=1, keepdims=True) > 0.5
    newest = jnp.dot(
        chosen.astype(jnp.bfloat16), new_ref[...].reshape(sections * TILE_ROWS, width),
        preferred_element_type=jnp.float32)
    old = grad_ref[...].reshape(span, width).astype(jnp.float32)
    in_grad_ref[0] = jnp.where(hit, newest, old).astype(jnp.bfloat16).reshape(grad_ref.shape)


def per_device(sections, peers, out_grad, x_rows, saved_u, w_up_t, w_down, gate, route_tokens, route_count):
    micro, tokens, features = out_grad.shape
    cap = gate.shape[2]
    slots = micro * cap
    fold = TILE_ROWS // slots
    width = features // fold
    hid = w_down.shape[1]
    rows = peers * TILE_ROWS
    sizes = (sections, peers, micro, cap)

    vmem = pl.BlockSpec(memory_space=pltpu.VMEM)
    hbm = pl.BlockSpec(memory_space=pl.ANY)
    dma = pltpu.SemaphoreType.DMA
    half = rows // 2
    chips = peers // 2
    all_rows = peers * slots
    all_new, picks, scaled, hidden_t, activation_t = pl.pallas_call(
        functools.partial(chain_kernel, sizes),
        out_shape=(
            jax.ShapeDtypeStruct((sections, TILE_ROWS, width), jnp.bfloat16),
            jax.ShapeDtypeStruct((micro * tokens, sections * TILE_ROWS), jnp.float32),
            jax.ShapeDtypeStruct((all_rows, features), jnp.bfloat16),
            jax.ShapeDtypeStruct((hid, all_rows), jnp.bfloat16),
            jax.ShapeDtypeStruct((hid, all_rows), jnp.bfloat16),
        ),
        in_specs=[hbm] * 7,
        out_specs=(vmem,) * 5,
        scratch_shapes=[
            pltpu.SMEM(route_tokens.shape, jnp.int32),
            pltpu.SMEM(gate.shape, jnp.float32),
            pltpu.SMEM((1, 1, micro), jnp.int32),
            pltpu.VMEM(out_grad.shape, jnp.bfloat16),
            pltpu.VMEM(saved_u.shape, jnp.bfloat16),
            pltpu.VMEM((hid, features), jnp.bfloat16),
            pltpu.VMEM((hid, features), jnp.bfloat16),
            pltpu.VMEM((rows, width), jnp.bfloat16),
            pltpu.VMEM((rows, width), jnp.bfloat16),
            pltpu.VMEM((half, width), jnp.bfloat16),
            pltpu.VMEM((half, width), jnp.bfloat16),
            pltpu.VMEM((half, width), jnp.bfloat16),
            pltpu.VMEM((sections, TILE_ROWS, width), jnp.bfloat16),
            pltpu.VMEM((sections, 8, 128), jnp.int32),
            pltpu.VMEM((TILE_ROWS, width), jnp.float32),
            pltpu.VMEM((rows, hid), jnp.float32),
            dma((7,)),
            dma((CHUNKS, chips)),
            dma((CHUNKS, chips)),
            dma((CHUNKS,)),
            dma((CHUNKS,)),
            dma((CHUNKS,)),
            dma((CHUNKS,)),
            dma((CHUNKS, chips)),
            dma((CHUNKS, chips)),
            dma((sections,)),
            dma((sections,)),
            dma((CHUNKS, sections)),
            dma((CHUNKS, sections)),
        ],
        compiler_params=pltpu.CompilerParams(
            collective_id=0, has_side_effects=True, vmem_limit_bytes=60 * 1024 * 1024),
    )(route_tokens, gate, route_count.transpose(0, 2, 1), out_grad, saved_u, w_up_t, w_down)

    per_piece = 3
    block = width // per_piece
    return pl.pallas_call(
        functools.partial(gradient_kernel, (sections, slots, per_piece)),
        grid=(fold * per_piece,),
        out_shape=(
            jax.ShapeDtypeStruct((1, micro, tokens, features), jnp.bfloat16),
            jax.ShapeDtypeStruct((1, hid, features), jnp.bfloat16),
            jax.ShapeDtypeStruct((1, hid, features), jnp.bfloat16),
        ),
        in_specs=[
            pl.BlockSpec((hid, all_rows), lambda i: (0, 0)),
            pl.BlockSpec((hid, all_rows), lambda i: (0, 0)),
            pl.BlockSpec((all_rows, block), lambda i: (0, i)),
            pl.BlockSpec((1, micro, peers * cap, block), lambda i: (0, 0, 0, i)),
            pl.BlockSpec((micro, tokens, block), lambda i: (0, 0, i)),
            pl.BlockSpec((sections, TILE_ROWS, block), lambda i: (0, 0, i % per_piece)),
            pl.BlockSpec((micro * tokens, sections * TILE_ROWS), lambda i: (0, 0)),
        ],
        out_specs=(
            pl.BlockSpec((1, micro, tokens, block), lambda i: (0, 0, 0, i)),
            pl.BlockSpec((1, hid, block), lambda i: (0, 0, i)),
            pl.BlockSpec((1, hid, block), lambda i: (0, 0, i)),
        ),
        compiler_params=pltpu.CompilerParams(vmem_limit_bytes=60 * 1024 * 1024),
    )(hidden_t, activation_t, scaled, x_rows, out_grad, all_new, picks)


def solution(mesh):
    return jax.shard_map(
        functools.partial(per_device, mesh.shape["section"], mesh.shape["dp"]),
        mesh=mesh,
        in_specs=(
            P(None, "dp", None),
            P("section", None, None, None),
            P("section", None, None, "dp"),
            P("section", "dp", None),
            P("section", "dp", None),
            P("section", None, "dp"),
            P("section", None, "dp"),
            P("section", None, "dp"),
        ),
        out_specs=(
            P("section", None, "dp", None),
            P("section", "dp", None),
            P("section", "dp", None),
        ),
        check_vma=False,
    )
```
